256 devices in a mesh: tgroup: 8 (over z), chan: 32 (over y, x, core).
Axes of the slice: x: 4, y: 4, z: 8, core: 2. Of those that a mesh axis runs over, the one named last changes fastest.
Arguments:
- raw_strain: float32 [32768, 10240], P(('tgroup', 'chan')), may hold values from -6 to 6
- whitening_taps: float32 [255], replicated, may hold values from -0.375 to 0.375
- first_block: int32 [64], P('chan'), may hold values from 0 to 39, as said below
- pair_owner: int32 [512, 1], P('chan'), may hold values from 0 to 7; in each aligned block of 16 rows (0 to 15, 16 to 31, ...) at most 5 rows name the same one
Outputs:
- stacks: float32 [1280, 8, 8, 1001], P(('tgroup', 'chan'))
The draws below stay inside these ranges and needn't reach their ends.
Inputs may be any that keep to these rules, and one draw needn't show every extreme that they name: `first_block`: each chan index lists 2 stripes; its first stripe starts within the last 7 of its 40 blocks; chan index 0 lists block 39 first and block 0 second. `pair_owner`: pair blocks are ordered by chan index, stripe, then partner offset. Among the 16 pair blocks of one chan index at most 5 share an owner, and exactly 5 do in some chan index.
All inputs are finite; a program needn't handle non-finite values.
Results may differ from the reference program's by a relative error of at most 0.02.
Values may be sent and summed in bfloat16 or wider, within the bound.
A program may use at most 128 MiB of HBM per device.

```python
import math
import jax
import jax.numpy as jnp
import numpy as np
from jax import lax

CHANNELS = 10240
TAPS = 255
MAXLAG = 500
CB = 8
K = 8
STRIPES = 2
SLOTS = 5
TS = 4096
TD = 2048
LAGS = 1001
TIME = 32768
BPD = 40
N_TGROUP = 8
N_CHAN = 32


def draw_first_block(key, part):
    key = jax.random.fold_in(key, 11)
    key_near, key_rest = jax.random.split(key)
    near = jax.random.randint(key_near, (N_CHAN, 1), BPD - K + 1, BPD)
    remaining = jax.random.randint(key_rest, (N_CHAN, STRIPES - 1), 0, BPD)
    near = near.at[0, 0].set(BPD - 1)
    remaining = remaining.at[0, 0].set(0)
    return jnp.concatenate([near, remaining], 1).reshape(N_CHAN * STRIPES).astype(jnp.int32)


def level_of(rng, dims, cuts, smallest, largest):
    level, own = 1.0, jax.random.fold_in(rng, 6)
    for axis_at, shards_of in cuts:
        steps = jnp.exp(jax.random.uniform(jax.random.fold_in(own, axis_at), (shards_of,), jnp.float32, smallest / len(cuts), largest / len(cuts)))
        level = level * jnp.repeat(steps, dims[axis_at] // shards_of).reshape([-1 if axis == axis_at else 1 for axis in range(len(dims))])
    return level


def deal_out(stream_key, own, number, rows, count, top, bound, slope):
    ranking = jax.random.permutation(stream_key, count)
    crowded, usual = portions_of(count, rows * top, bound, slope, True), portions_of(count, rows * top, bound, slope, False)
    places = jnp.arange(count)

    def named(lengths, offset_by):
        used = int((lengths > 0).sum())
        fixed = max(1, used // 4)
        shifted = fixed + (places - fixed + offset_by * (used - fixed)) % max(1, count - fixed)
        return jnp.zeros((count,), jnp.int32).at[ranking[jnp.where(places < fixed, places, shifted)]].set(jnp.asarray(lengths, jnp.int32))

    lengths = jnp.where(number % 4 == 0, named(crowded, number // 4), named(usual, number - number // 4 - 1))
    mixed = jax.random.permutation(jax.random.fold_in(own, 3), count)
    donor, sink = mixed[0:count // 2 * 2:2], mixed[1:count // 2 * 2:2]
    margin = jnp.minimum(lengths[donor] - 1, bound - lengths[sink]) // 2
    margin = jnp.where((donor == ranking[0]) | (sink == ranking[0]) | (lengths[sink] == 0), 0, jnp.maximum(margin, 0))
    shifted = jax.random.randint(jax.random.fold_in(own, 4), (count // 2,), 0, 1 << 20) % (margin + 1)
    lengths = lengths.at[donor].add(-shifted).at[sink].add(shifted)
    labels = jnp.searchsorted(jnp.cumsum(lengths), jnp.arange(rows * top), side="right").astype(jnp.int32)
    table = labels.reshape(top, rows).T
    table = table[jax.random.permutation(jax.random.fold_in(own, 1), rows)]
    offset_by = jax.random.randint(jax.random.fold_in(own, 2), (rows, 1), 0, top)
    return jnp.take_along_axis(table, (jnp.arange(top)[None, :] + offset_by) % top, axis=1)


def portions_of(number_of, total, reach, slope, full):
    weights = [(1 << 20) // math.isqrt(rank ** slope) + 1 for rank in range(1, number_of + 1)]
    largest = reach if full else min(reach, max(-(-total // number_of), total * weights[0] // sum(weights)))
    least = 1 if total - largest >= number_of - 1 else 0
    holding, spare = [largest] + [least] * (number_of - 1), total - largest - least * (number_of - 1)
    while spare > 0:
        movable = [i for i in range(1, number_of) if holding[i] < largest] or [i for i in range(1, number_of) if holding[i] < reach]
        pool, budget = sum([weights[i] for i in movable]), spare
        for i in movable:
            extra = min(reach - holding[i], max(1, budget * weights[i] // pool), spare)
            holding[i] = holding[i] + extra
            spare = spare - extra
    return np.array(holding)


def centred(stream_key, dims, scale, most, pieces=(), kind=jnp.bfloat16):
    factor_of = level_of(stream_key, dims, pieces, -0.22, 0.18) if pieces else 1.0
    drawn = jax.random.normal(stream_key, dims, jnp.float32) * scale * factor_of
    return jnp.minimum(jnp.maximum(drawn, -most), most).astype(kind)


def setup_inputs(seed: int = 0) -> dict:
    keys = jax.random.split(jax.random.key(seed), 5)
    raw_strain = centred(keys[0], (TIME, CHANNELS), 1.0, 6.0, ((0, 256),), jnp.float32)
    whitening_taps = centred(keys[1], (TAPS,), TAPS ** -0.5, 0.375, (), jnp.float32)
    first_block = draw_first_block(jax.random.fold_in(keys[4], 71), 0)
    pair_owner_keys = jax.random.split(jax.random.fold_in(keys[3], 1), (N_CHAN * STRIPES * K) // (STRIPES * K))
    pair_owner_turns = jax.random.permutation(jax.random.fold_in(keys[3], 3), (N_CHAN * STRIPES * K) // (STRIPES * K))
    pair_owner = jax.vmap(lambda own, number: deal_out(jax.random.fold_in(keys[3], 2), own, number, STRIPES * K, N_TGROUP, 1, SLOTS, 2))(pair_owner_keys, pair_owner_turns).reshape((N_CHAN * STRIPES * K, 1))
    return {"raw_strain": raw_strain, "whitening_taps": whitening_taps, "first_block": first_block, "pair_owner": pair_owner}


def whiten_segment(segment, whitening_taps):
    series = segment.T
    fft_length = 1 << (TS + TAPS).bit_length()
    reversed_taps = jnp.flip(whitening_taps)
    spectrum = jnp.fft.rfft(series, n=fft_length, axis=1) * jnp.fft.rfft(reversed_taps, n=fft_length)[None, :]
    convolved = jnp.fft.irfft(spectrum, n=fft_length, axis=1)
    half_taps = (TAPS - 1) // 2
    return convolved[:, half_taps:half_taps + TS:2].astype(jnp.bfloat16)

def correlate_segment(filtered, first_block):
    extended = jnp.concatenate([filtered.astype(jnp.float32), jnp.zeros(((K - 1) * CB, TD), jnp.float32)], 0)
    fft_length = 1 << (TD + LAGS).bit_length()
    spectra = jnp.fft.rfft(extended, n=fft_length, axis=1)
    column_starts = jnp.arange(N_CHAN * STRIPES, dtype=jnp.int32) // STRIPES * (CHANNELS // N_CHAN) + first_block * CB
    factor = 1.0 / math.sqrt(TD)

    def one_stripe(offset_row):
        leading = lax.dynamic_slice_in_dim(spectra, offset_row, CB, 0)
        partners = lax.dynamic_slice_in_dim(spectra, offset_row, K * CB, 0)
        cross = jnp.conj(leading)[:, None, :] * partners[None, :, :]
        circular = jnp.fft.irfft(cross, n=fft_length, axis=2)
        lagged = jnp.concatenate([circular[:, :, fft_length - MAXLAG:], circular[:, :, :MAXLAG + 1]], 2)
        scaled = (lagged * factor).astype(jnp.bfloat16)
        return scaled.reshape(CB, K, CB, LAGS).transpose(1, 0, 2, 3)
    stacked = lax.map(one_stripe, column_starts.astype(jnp.int32))
    return stacked.reshape(N_CHAN * STRIPES * K, CB, CB, LAGS)

def reference(raw_strain, whitening_taps, first_block, pair_owner):
    segments = raw_strain.reshape(N_TGROUP, TS, CHANNELS)

    def accumulate(running, segment):
        filtered = whiten_segment(segment, whitening_taps)
        partial_value = correlate_segment(filtered, first_block)
        return (running + partial_value.astype(jnp.float32), None)
    pair_total = N_CHAN * STRIPES * K
    summed = lax.scan(accumulate, jnp.zeros((pair_total, CB, CB, LAGS), jnp.float32), segments)[0]
    owners_grid = pair_owner[:, 0].reshape(N_CHAN, STRIPES * K)
    owner_hot = (owners_grid[:, :, None] == jnp.arange(N_TGROUP, dtype=jnp.int32)[None, None, :]).astype(jnp.int32)
    earlier = jnp.cumsum(owner_hot, axis=1) - owner_hot
    slot_index = lax.optimization_barrier(jnp.sum(earlier * owner_hot, axis=2))
    column = jnp.arange(N_CHAN, dtype=jnp.int32)[:, None]
    target = ((owners_grid * N_CHAN + column) * SLOTS + slot_index).reshape(pair_total).astype(jnp.int32)
    stacks = jnp.zeros((N_TGROUP * N_CHAN * SLOTS, CB, CB, LAGS), jnp.float32).at[target].set(summed)
    return stacks
```

```python
import math

import jax
import jax.numpy as jnp
from jax import lax
from jax.experimental import pallas as pl
from jax.experimental.pallas import tpu as pltpu
from jax.sharding import PartitionSpec as P

MESH = pl.DeviceIdType.MESH
MAXLAG = 500
LAGS = 1001
CB = 8
K = 8
STRIPES = 2
SLOTS = 5
TAPS = 255
NG = 8
NC = 32
CPD = 320
CHANNELS = 10240
ROWS = 128
TS = 4096
TD = 2048
PAIRS = STRIPES * K
WIDE = CHANNELS + 128
FB = 256
FW = 768
R = 32
KL = TD + 128
SPAN = 384
QW = TD + 1024
F32 = jnp.float32
BF = jnp.bfloat16


def chan_copy(send_ref, x_ref, send_sem, recv_sem, dst, src):
    return pltpu.make_async_remote_copy(
        src_ref=send_ref.at[dst],
        dst_ref=x_ref.at[1 + src],
        send_sem=send_sem.at[dst],
        recv_sem=recv_sem.at[src],
        device_id={"chan": dst},
        device_id_type=MESH,
    )


def first_copy(fb_ref, table_ref, send_sem, recv_sem, dst, src):
    return pltpu.make_async_remote_copy(
        src_ref=fb_ref.at[0],
        dst_ref=table_ref.at[src],
        send_sem=send_sem.at[dst],
        recv_sem=recv_sem.at[src],
        device_id={"chan": dst},
        device_id_type=MESH,
    )


def group_copy(src_ref, dst_ref, send_sem, recv_sem, dst, src):
    return pltpu.make_async_remote_copy(
        src_ref=src_ref,
        dst_ref=dst_ref.at[src],
        send_sem=send_sem.at[dst],
        recv_sem=recv_sem.at[src],
        device_id={"tgroup": dst},
        device_id_type=MESH,
    )


def kernel(
    raw_ref, taps_ref, fb_ref, owner_ref, out_ref,
    raw_v, by_chan, table_v, fb_v, send_v, x_v, filt, zsend, zrecv, leads, lead_f, shifted, windows, acc,
    raw_sem, fsend, frecv, csend, crecv, zs, zr, ls, lr,
):
    me_c = lax.axis_index("chan")
    me_g = lax.axis_index("tgroup")

    barrier = pltpu.get_barrier_semaphore()

    def greet_chan(d, carry):
        pl.semaphore_signal(barrier, inc=1, device_id={"chan": lax.rem(me_c + d, NC)}, device_id_type=MESH)
        return carry

    def greet_group(d, carry):
        pl.semaphore_signal(barrier, inc=1, device_id={"tgroup": lax.rem(me_g + d, NG)}, device_id_type=MESH)
        return carry

    lax.fori_loop(1, NC, greet_chan, 0)
    lax.fori_loop(1, NG, greet_group, 0)

    raw_in = pltpu.make_async_copy(raw_ref, raw_v, raw_sem)
    raw_in.start()
    lane = lax.broadcasted_iota(jnp.int32, (8, 128), 1)
    fb_v[0] = jnp.where(lane == 0, fb_ref[0], jnp.where(lane == 1, fb_ref[1], 0))
    table_v[me_c] = fb_v[0]
    by_chan[pl.ds(CHANNELS, 128)] = jnp.zeros((128, ROWS), BF)
    x_v[0] = jnp.zeros((128, ROWS), BF)
    x_v[NC + 1] = jnp.zeros((128, ROWS), BF)
    lead_f[:, pl.ds(TD, 128)] = jnp.zeros((STRIPES * CB, 128), F32)
    acc[...] = jnp.zeros_like(acc)
    pl.semaphore_wait(barrier, NC + NG - 2)

    def send_first(d, carry):
        first_copy(fb_v, table_v, fsend, frecv, lax.rem(me_c + d, NC), me_c).start()
        return carry

    def wait_first(d, carry):
        first_copy(fb_v, table_v, fsend, frecv, lax.rem(me_c + d, NC), lax.rem(me_c + NC - d, NC)).wait_recv()
        return carry

    def wait_first_sent(d, carry):
        first_copy(fb_v, table_v, fsend, frecv, lax.rem(me_c + d, NC), me_c).wait_send()
        return carry

    lax.fori_loop(1, NC, send_first, 0)
    raw_in.wait()

    def turn_over(i, carry):
        at = pl.multiple_of(i * 128, 128)
        by_chan[pl.ds(at, 128)] = raw_v[:, pl.ds(at, 128)].T.astype(BF)
        return carry

    lax.fori_loop(0, CHANNELS // 128, turn_over, 0)

    band = pltpu.roll(jnp.broadcast_to(taps_ref[...], (FB, FW)), 0, 1, stride=2, stride_axis=0)
    band_hi = band.astype(BF)
    band_lo = (band - band_hi.astype(F32)).astype(BF)

    owners = [owner_ref[q, 0] for q in range(PAIRS)]
    slots = []
    for q in range(PAIRS):
        count = jnp.int32(0)
        for earlier in range(q):
            count = count + jnp.where(owners[earlier] == owners[q], 1, 0)
        slots.append(count)
    lane_row = lax.broadcasted_iota(jnp.int32, (1, 128), 1)
    target = jnp.zeros((1, 128), jnp.int32)
    for q in range(PAIRS):
        target = jnp.where(lane_row // CB == q, owners[q] * SLOTS + slots[q], target)
    stripe_of = []
    for s in range(SLOTS):
        value = jnp.int32(0)
        for q in range(K, PAIRS):
            value = value + jnp.where((owners[q] == me_g) & (slots[q] == s), 1, 0)
        stripe_of.append(value)

    lax.fori_loop(1, NC, wait_first, 0)

    pick_row = lax.broadcasted_iota(jnp.int32, (128, SPAN), 0)
    pick_col = lax.broadcasted_iota(jnp.int32, (128, SPAN), 1)
    offset = pick_col - pick_row % (K * CB)

    def packed(dst):
        firsts = table_v[dst]
        wanted = jnp.where(pick_row < K * CB, firsts[:1, :1], firsts[:1, 1:2]) * CB
        source = by_chan[pl.ds(pl.multiple_of(dst * CPD, K * CB), SPAN)]
        chosen = jnp.where(offset == wanted, 1.0, 0.0).astype(BF)
        return jnp.dot(chosen, source, preferred_element_type=F32).astype(BF)

    def send_packed(d, carry):
        dst = lax.rem(me_c + d, NC)
        send_v[dst] = packed(dst)
        chan_copy(send_v, x_v, csend, crecv, dst, me_c).start()
        return carry

    lax.fori_loop(1, NC, send_packed, 0)
    x_v[1 + me_c] = packed(me_c)

    def wait_packed(d, carry):
        chan_copy(send_v, x_v, csend, crecv, lax.rem(me_c + d, NC), lax.rem(me_c + NC - d, NC)).wait_recv()
        return carry

    lax.fori_loop(1, NC, wait_packed, 0)

    for block in range(TD // FB):
        window = jnp.concatenate([x_v[4 * block + part] for part in range(FW // ROWS)], 1)
        y = sum(
            lax.dot_general(window, term, (((1,), (1,)), ((), ())), preferred_element_type=F32)
            for term in (band_hi, band_lo)
        )
        filt[:, pl.ds(block * FB, FB)] = y.astype(BF)

    rows = NG * SLOTS * CB
    row_id = lax.broadcasted_iota(jnp.int32, (rows, 128), 0)
    col_id = lax.broadcasted_iota(jnp.int32, (rows, 128), 1)
    pick = (jnp.broadcast_to(target, (rows, 128)) == row_id // CB) & (row_id % CB == col_id % CB)
    chosen = jnp.dot(jnp.where(pick, 1.0, 0.0).astype(BF), filt[...], preferred_element_type=F32)
    for owner in range(NG):
        part = chosen[owner * SLOTS * CB:(owner + 1) * SLOTS * CB]
        zsend[owner] = jnp.concatenate([part[:, :TD // 2], part[:, TD // 2:]], 0).astype(BF)
    lead_rows = jnp.concatenate([filt[pl.ds(0, 16)].astype(F32)[:CB], filt[pl.ds(K * CB, 16)].astype(F32)[:CB]], 0)
    leads[me_g] = lead_rows.astype(BF)
    zrecv[me_g] = zsend[me_g]

    def step_offset(i):
        return jnp.where(i % 2 == 1, (i + 1) // 2, NG - i // 2)

    def send_group(i, carry):
        dst = lax.rem(me_g + step_offset(i), NG)
        group_copy(leads.at[me_g], leads, ls, lr, dst, me_g).start()
        group_copy(zsend.at[dst], zrecv, zs, zr, dst, me_g).start()
        return carry

    lax.fori_loop(1, NG, send_group, 0)

    def correlate(src):
        lead_f[:, pl.ds(0, TD)] = leads[src].astype(F32)
        for row in range(STRIPES * CB):
            line = jnp.broadcast_to(lead_f[pl.ds(row, 1)], (R, KL))
            turned = pltpu.roll(line, 0, 1, stride=1, stride_axis=0)
            shifted[row // CB, pl.ds(row % CB * R, R)] = turned.astype(BF)
        halves = zrecv[src].astype(F32)
        width = SLOTS * CB
        padded = jnp.concatenate([halves[:width], halves[width:], jnp.zeros((width, QW - TD), F32)], 1)
        turns = [pltpu.roll(padded, MAXLAG - R * step, 1) for step in range(128 // R)]
        for slot in range(SLOTS):
            windows[slot] = jnp.concatenate([turn[slot * CB:(slot + 1) * CB] for turn in turns], 0).astype(BF)
        for slot in range(SLOTS):
            partner = jnp.concatenate(
                [windows[slot, :, pl.ds(128 * step, KL)] for step in range(1024 // 128)], 0
            )
            acc[slot] += lax.dot_general(
                partner, shifted[stripe_of[slot]], (((1,), (1,)), ((), ())), preferred_element_type=F32
            )

    correlate(me_g)

    def receive(i, carry):
        src = lax.rem(me_g + NG - step_offset(i), NG)
        group_copy(leads.at[me_g], leads, ls, lr, src, src).wait_recv()
        group_copy(zsend.at[src], zrecv, zs, zr, src, src).wait_recv()
        correlate(src)
        return carry

    lax.fori_loop(1, NG, receive, 0)

    scale = 1.0 / math.sqrt(TD)
    quarter = lax.broadcasted_iota(jnp.int32, (CB, 128), 1) // R

    def finish(slot, carry):
        for step in range(1024 // 128):
            for half in range(2):
                pieces = [
                    acc[slot, pl.ds(step * 4 * CB + s * CB, CB), pl.ds(half * 128, 128)] * scale
                    for s in range(4)
                ]
                for a in range(4):
                    value = pieces[a]
                    for s in range(4):
                        if s != a:
                            value = jnp.where(quarter == s, pltpu.roll(pieces[s], (s - a) * R % 128, 1), value)
                    width = min(128, LAGS - step * 128)
                    out_ref[slot, half * 4 + a, :, pl.ds(step * 128, width)] = value[:, :width]
        return carry

    lax.fori_loop(0, SLOTS, finish, 0)

    lax.fori_loop(1, NC, wait_first_sent, 0)

    def wait_packed_sent(d, carry):
        chan_copy(send_v, x_v, csend, crecv, lax.rem(me_c + d, NC), me_c).wait_send()
        return carry

    lax.fori_loop(1, NC, wait_packed_sent, 0)

    def wait_group_sent(i, carry):
        dst = lax.rem(me_g + step_offset(i), NG)
        group_copy(leads.at[me_g], leads, ls, lr, dst, me_g).wait_send()
        group_copy(zsend.at[dst], zrecv, zs, zr, dst, me_g).wait_send()
        return carry

    lax.fori_loop(1, NG, wait_group_sent, 0)


def local(raw_strain, whitening_taps, first_block, pair_owner):
    taps = jnp.pad(whitening_taps, (1, FW - TAPS - 1)).reshape(1, FW)
    vmem = pl.BlockSpec(memory_space=pltpu.VMEM)
    smem = pl.BlockSpec(memory_space=pltpu.SMEM)
    dma = pltpu.SemaphoreType.DMA
    return pl.pallas_call(
        kernel,
        out_shape=jax.ShapeDtypeStruct((SLOTS, CB, CB, LAGS), F32),
        in_specs=[pl.BlockSpec(memory_space=pl.ANY), vmem, smem, smem],
        out_specs=vmem,
        scratch_shapes=[
            pltpu.VMEM((ROWS, CHANNELS), F32),
            pltpu.VMEM((WIDE, ROWS), BF),
            pltpu.VMEM((NC, 8, 128), jnp.int32),
            pltpu.VMEM((1, 8, 128), jnp.int32),
            pltpu.VMEM((NC, ROWS, 128), BF),
            pltpu.VMEM((NC + 2, 128, ROWS), BF),
            pltpu.VMEM((128, TD), BF),
            pltpu.VMEM((NG, 2 * SLOTS * CB, TD // 2), BF),
            pltpu.VMEM((NG, 2 * SLOTS * CB, TD // 2), BF),
            pltpu.VMEM((NG, STRIPES * CB, TD), BF),
            pltpu.VMEM((STRIPES * CB, KL), F32),
            pltpu.VMEM((STRIPES, CB * R, KL), BF),
            pltpu.VMEM((SLOTS, 4 * CB, QW), BF),
            pltpu.VMEM((SLOTS, 256, 256), F32),
            dma, dma((NC,)), dma((NC,)), dma((NC,)), dma((NC,)),
            dma((NG,)), dma((NG,)), dma((NG,)), dma((NG,)),
        ],
        compiler_params=pltpu.CompilerParams(
            collective_id=0, has_side_effects=True, vmem_limit_bytes=56 << 20
        ),
        cost_estimate=pl.CostEstimate(flops=12 << 30, bytes_accessed=8 << 20, transcendentals=0),
    )(raw_strain, taps, first_block, pair_owner)


def solution(mesh):
    in_specs = (P(("tgroup", "chan"), None), P(), P("chan"), P("chan", None))
    out_specs = P(("tgroup", "chan"), None, None, None)
    return jax.shard_map(local, mesh=mesh, in_specs=in_specs, out_specs=out_specs, check_vma=False)
```

```python
import math

import jax
import jax.numpy as jnp
from jax import lax
from jax.experimental import pallas as pl
from jax.experimental.pallas import tpu as pltpu
from jax.sharding import PartitionSpec as P

MESH = pl.DeviceIdType.MESH
MAXLAG = 500
LAGS = 1001
CB = 8
K = 8
STRIPES = 2
SLOTS = 5
TAPS = 255
NG = 8
NC = 32
CPD = 320
CHANNELS = 10240
ROWS = 128
TS = 4096
TD = 2048
HALF = TD // 2
PAIRS = STRIPES * K
WIDE = CHANNELS + 128
SPAN = 512
EARLY = 80
FB = 256
FW = 768
R = 32
KL = TD + 128
QW = TD + 1024
F32 = jnp.float32
BF = jnp.bfloat16
I32 = jnp.int32


def remote(src, dst, send_sem, recv_sem, axis, target):
    return pltpu.make_async_remote_copy(
        src_ref=src, dst_ref=dst, send_sem=send_sem, recv_sem=recv_sem,
        device_id={axis: target}, device_id_type=MESH,
    )


def kernel(
    raw_ref, taps_ref, fb_ref, owner_ref, acc,
    raw_v, raw_b, table_v, mine_v, send_v, x_v, filt, send0, recv0, send1, recv1, leads, lead_f, shifted, windows,
    raw_sem, fsend, frecv, asend, arecv, bsend, brecv, s0, r0, s1, r1, ls, lr,
):
    me_c = lax.axis_index("chan")
    me_g = lax.axis_index("tgroup")

    barrier = pltpu.get_barrier_semaphore()

    def greet_chan(d, carry):
        pl.semaphore_signal(barrier, inc=1, device_id={"chan": lax.rem(me_c + d, NC)}, device_id_type=MESH)
        return carry

    def greet_group(d, carry):
        pl.semaphore_signal(barrier, inc=1, device_id={"tgroup": lax.rem(me_g + d, NG)}, device_id_type=MESH)
        return carry

    lax.fori_loop(1, NC, greet_chan, 0)
    lax.fori_loop(1, NG, greet_group, 0)
    raw_in = pltpu.make_async_copy(raw_ref, raw_v, raw_sem)
    raw_in.start()

    owners = [owner_ref[q] for q in range(PAIRS)]
    slots = []
    for q in range(PAIRS):
        count = jnp.int32(0)
        for earlier in range(q):
            count = count + jnp.where(owners[earlier] == owners[q], 1, 0)
        slots.append(count)
    keys = [jnp.int32(q // K - 2) if q % K == 0 else slots[q] * PAIRS + q for q in range(PAIRS)]
    places = [jnp.int32(0)] * PAIRS
    for q in range(PAIRS):
        for other in range(q):
            ahead = jnp.where(keys[other] < keys[q], 1, 0)
            places[q] = places[q] + ahead
            places[other] = places[other] + 1 - ahead
    place_row = lax.broadcasted_iota(I32, (PAIRS, 128), 0)
    place_lane = lax.broadcasted_iota(I32, (1, 128), 1) // CB
    starts = jnp.zeros((PAIRS, 128), I32)
    target = jnp.zeros((1, 128), I32)
    for q in range(PAIRS):
        starts = jnp.where(place_row == places[q], (fb_ref[q // K] + q % K) * CB, starts)
        target = jnp.where(place_lane == places[q], owners[q] * SLOTS + slots[q], target)
    mine_v[...] = starts
    table_v[me_c] = starts
    stripe_of = []
    for s in range(SLOTS):
        value = jnp.int32(0)
        for q in range(K, PAIRS):
            value = value + jnp.where((owners[q] == me_g) & (slots[q] == s), 1, 0)
        stripe_of.append(value)

    raw_b[:, pl.ds(CHANNELS, 128)] = jnp.zeros((ROWS, 128), BF)
    x_v[0] = jnp.zeros((128, ROWS), BF)
    x_v[NC + 1] = jnp.zeros((128, ROWS), BF)
    lead_f[:, pl.ds(TD, 128)] = jnp.zeros((STRIPES * CB, 128), F32)

    pl.semaphore_wait(barrier, NC + NG - 2)

    def first_copy(d, peer, owner):
        return remote(mine_v, table_v.at[owner], fsend.at[d], frecv.at[d], "chan", peer)

    def send_first(d, carry):
        first_copy(d, lax.rem(me_c + d, NC), me_c).start()
        return carry

    lax.fori_loop(1, NC, send_first, 0)

    line = jnp.concatenate([taps_ref[...].reshape(1, TAPS), jnp.zeros((1, FW - TAPS), F32)], 1)
    band = pltpu.roll(jnp.broadcast_to(line, (FB, FW)), 1, 1, stride=2, stride_axis=0)
    band_hi = band.astype(BF)
    band_lo = (band - band_hi.astype(F32)).astype(BF)

    raw_in.wait()

    def round_raw(i, carry):
        at = pl.multiple_of(i * 512, 512)
        raw_b[:, pl.ds(at, 512)] = raw_v[:, pl.ds(at, 512)].astype(BF)
        return carry

    lax.fori_loop(0, CHANNELS // 512, round_raw, 0)

    def wait_first(d, carry):
        peer = lax.rem(me_c + NC - d, NC)
        first_copy(d, peer, peer).wait_recv()
        return carry

    lax.fori_loop(1, NC, wait_first, 0)

    ahead_by = lax.broadcasted_iota(I32, (CB, SPAN), 1) - lax.broadcasted_iota(I32, (CB, SPAN), 0)

    def packed(dst):
        base = (dst * CPD) // 128 * 128
        shift = dst * CPD - base
        hot = []
        for place in range(PAIRS):
            wanted = jnp.broadcast_to(table_v[dst, pl.ds(place, 1), :] + shift, (CB, 128))
            hot.append(jnp.where(ahead_by == jnp.concatenate([wanted] * (SPAN // 128), 1), 1.0, 0.0))
        chosen = jnp.concatenate(hot, 0).astype(BF)
        source = raw_b[:, pl.ds(pl.multiple_of(base, 128), SPAN)]
        return lax.dot_general(chosen, source, (((1,), (1,)), ((), ())), preferred_element_type=F32).astype(BF)

    def early_copy(d, dst, src):
        return remote(
            send_v.at[dst, pl.ds(0, EARLY)], x_v.at[1 + src, pl.ds(0, EARLY)], asend.at[d], arecv.at[d], "chan", dst
        )

    def late_copy(d, dst, src):
        return remote(
            send_v.at[dst, pl.ds(EARLY, 128 - EARLY)], x_v.at[1 + src, pl.ds(EARLY, 128 - EARLY)],
            bsend.at[d], brecv.at[d], "chan", dst,
        )

    def send_early(d, carry):
        dst = lax.rem(me_c + d, NC)
        send_v[dst] = packed(dst)
        early_copy(d, dst, me_c).start()
        return carry

    def send_late(d, carry):
        late_copy(d, lax.rem(me_c + d, NC), me_c).start()
        return carry

    lax.fori_loop(1, NC, send_early, 0)
    lax.fori_loop(1, NC, send_late, 0)
    x_v[1 + me_c] = packed(me_c)

    def wait_early(d, carry):
        peer = lax.rem(me_c + NC - d, NC)
        early_copy(d, peer, peer).wait_recv()
        return carry

    def wait_late(d, carry):
        peer = lax.rem(me_c + NC - d, NC)
        late_copy(d, peer, peer).wait_recv()
        return carry

    def whiten(at, count):
        window = jnp.concatenate(
            [
                jnp.concatenate([x_v[4 * block + part, pl.ds(at, count)] for part in range(FW // ROWS)], 1)
                for block in range(TD // FB)
            ],
            0,
        )
        y = sum(
            lax.dot_general(window, term, (((1,), (1,)), ((), ())), preferred_element_type=F32)
            for term in (band_hi, band_lo)
        )
        for block in range(TD // FB):
            filt[pl.ds(at, count), pl.ds(block * FB, FB)] = y[block * count:(block + 1) * count].astype(BF)

    def chosen_rows(first, count, depth):
        rows = NG * count * CB
        row_id = lax.broadcasted_iota(I32, (rows, depth), 0)
        col_id = lax.broadcasted_iota(I32, (rows, depth), 1)
        wanted = row_id // (count * CB) * SLOTS + first + row_id // CB % count
        pick = (jnp.broadcast_to(target[:, :depth], (rows, depth)) == wanted) & (row_id % CB == col_id % CB)
        rows_of = jnp.dot(
            jnp.where(pick, 1.0, 0.0).astype(BF), filt[pl.ds(0, depth)], preferred_element_type=F32
        )
        parts = [rows_of[o * count * CB:(o + 1) * count * CB] for o in range(NG)]
        return [jnp.concatenate([part[:, :HALF], part[:, HALF:]], 0).astype(BF) for part in parts]

    lax.fori_loop(1, NC, wait_early, 0)
    whiten(0, EARLY)

    right = lax.rem(me_g + 1, NG)
    left = lax.rem(me_g + NG - 1, NG)

    def lead_copy(way, hop):
        back = hop - 1 if way == 0 else NG - hop + 1
        origin = lax.rem(me_g + NG - back, NG)
        part = leads.at[origin] if hop < 4 else leads.at[origin, way]
        return remote(part, part, ls.at[way, hop - 1], lr.at[way, hop - 1], "tgroup", right if way == 0 else left)

    def lead_arrival(way, hop):
        back = hop if way == 0 else NG - hop
        origin = lax.rem(me_g + NG - back, NG)
        part = leads.at[origin] if hop < 4 else leads.at[origin, way]
        return remote(part, part, ls.at[way, hop - 1], lr.at[way, hop - 1], "tgroup", right if way == 0 else left)

    def pass_leads(hop):
        for way in range(2):
            lead_arrival(way, hop - 1).wait_recv()
            lead_copy(way, hop).start()

    for half in range(2):
        leads[me_g, half] = filt[pl.ds(0, STRIPES * CB), pl.ds(half * HALF, HALF)]
    for way in range(2):
        lead_copy(way, 1).start()

    def step_offset(i):
        return jnp.where(i % 2 == 1, (i + 1) // 2, NG - i // 2)

    def slot0_copy(i, dst, src):
        return remote(send0.at[dst], recv0.at[src], s0.at[i], r0.at[i], "tgroup", dst)

    def slot1_copy(i, dst, src):
        return remote(send1.at[dst], recv1.at[src], s1.at[i], r1.at[i], "tgroup", dst)

    def send_slot0(i, carry):
        slot0_copy(i, lax.rem(me_g + step_offset(i), NG), me_g).start()
        return carry

    def send_slot1(i, carry):
        slot1_copy(i, lax.rem(me_g + step_offset(i), NG), me_g).start()
        return carry

    for owner, part in enumerate(chosen_rows(0, 1, EARLY)):
        send0[owner] = part
    lax.fori_loop(1, NG, send_slot0, 0)
    recv0[me_g] = send0[me_g]

    def spread_leads(src):
        for half in range(2):
            lead_f[:, pl.ds(half * HALF, HALF)] = leads[src, half].astype(F32)
        for row in range(STRIPES * CB):
            line = jnp.broadcast_to(lead_f[pl.ds(row, 1)], (R, KL))
            turned = pltpu.roll(line, 0, 1, stride=1, stride_axis=0)
            shifted[row // CB, pl.ds(row % CB * R, R)] = turned.astype(BF)

    def correlate(halves, first, count, fresh=False):
        width = count * CB
        halves = halves.astype(F32)
        padded = jnp.concatenate([halves[:width], halves[width:], jnp.zeros((width, QW - TD), F32)], 1)
        turns = [pltpu.roll(padded, MAXLAG - R * step, 1) for step in range(128 // R)]
        for s in range(count):
            windows[first + s] = jnp.concatenate([turn[s * CB:(s + 1) * CB] for turn in turns], 0).astype(BF)
        for slot in range(first, first + count):
            partner = jnp.concatenate(
                [windows[slot, :, pl.ds(128 * step, KL)] for step in range(1024 // 128)], 0
            )
            product = lax.dot_general(
                partner, shifted[stripe_of[slot]], (((1,), (1,)), ((), ())), preferred_element_type=F32
            )
            acc[slot] = product if fresh else acc[slot] + product

    spread_leads(me_g)
    correlate(recv0[me_g], 0, 1, True)
    pass_leads(2)

    lax.fori_loop(1, NC, wait_late, 0)
    whiten(EARLY, 128 - EARLY)
    for owner, part in enumerate(chosen_rows(1, SLOTS - 1, 128)):
        send1[owner] = part
    pass_leads(3)
    lax.fori_loop(1, 5, send_slot1, 0)
    correlate(send1[me_g], 1, SLOTS - 1, True)
    pass_leads(4)
    lax.fori_loop(5, NG, send_slot1, 0)

    def receive(i, carry):
        src = lax.rem(me_g + NG - step_offset(i), NG)

        @pl.when(i == NG - 1)
        def _():
            for way in range(2):
                lead_arrival(way, 4).wait_recv()

        spread_leads(src)
        slot0_copy(i, src, src).wait_recv()
        slot1_copy(i, src, src).wait_recv()
        halves0 = recv0[src]
        halves1 = recv1[src]
        correlate(halves0, 0, 1)
        correlate(halves1, 1, SLOTS - 1)
        return carry

    lax.fori_loop(1, NG, receive, 0)

    def wait_chan_sent(d, carry):
        dst = lax.rem(me_c + d, NC)
        first_copy(d, dst, me_c).wait_send()
        early_copy(d, dst, me_c).wait_send()
        late_copy(d, dst, me_c).wait_send()
        return carry

    lax.fori_loop(1, NC, wait_chan_sent, 0)

    def wait_group_sent(i, carry):
        dst = lax.rem(me_g + step_offset(i), NG)
        slot0_copy(i, dst, me_g).wait_send()
        slot1_copy(i, dst, me_g).wait_send()
        return carry

    lax.fori_loop(1, NG, wait_group_sent, 0)
    for way in range(2):
        for hop in range(1, 5):
            lead_copy(way, hop).wait_send()


def finish(acc_ref, out_ref):
    scale = 1.0 / math.sqrt(TD)
    quarter = lax.broadcasted_iota(I32, (CB, 128), 1) // R
    for step in range(1024 // 128):
        for half in range(2):
            pieces = [
                acc_ref[0, pl.ds(step * 4 * CB + s * CB, CB), pl.ds(half * 128, 128)] * scale for s in range(4)
            ]
            for a in range(4):
                value = pieces[a]
                for s in range(4):
                    if s != a:
                        value = jnp.where(quarter == s, pltpu.roll(pieces[s], (s - a) * R % 128, 1), value)
                width = min(128, LAGS - step * 128)
                out_ref[0, half * 4 + a, :, pl.ds(step * 128, width)] = value[:, :width]


def local(raw_strain, whitening_taps, first_block, pair_owner):
    vmem = pl.BlockSpec(memory_space=pltpu.VMEM)
    smem = pl.BlockSpec(memory_space=pltpu.SMEM)
    dma = pltpu.SemaphoreType.DMA
    acc = pl.pallas_call(
        kernel,
        out_shape=jax.ShapeDtypeStruct((SLOTS, 256, 256), F32),
        in_specs=[pl.BlockSpec(memory_space=pl.ANY), vmem, smem, smem],
        out_specs=vmem,
        scratch_shapes=[
            pltpu.VMEM((ROWS, CHANNELS), F32),
            pltpu.VMEM((ROWS, WIDE), BF),
            pltpu.VMEM((NC, PAIRS, 128), I32),
            pltpu.VMEM((PAIRS, 128), I32),
            pltpu.VMEM((NC, 128, ROWS), BF),
            pltpu.VMEM((NC + 2, 128, ROWS), BF),
            pltpu.VMEM((128, TD), BF),
            pltpu.VMEM((NG, 2 * CB, HALF), BF),
            pltpu.VMEM((NG, 2 * CB, HALF), BF),
            pltpu.VMEM((NG, 2 * CB * (SLOTS - 1), HALF), BF),
            pltpu.VMEM((NG, 2 * CB * (SLOTS - 1), HALF), BF),
            pltpu.VMEM((NG, 2, STRIPES * CB, HALF), BF),
            pltpu.VMEM((STRIPES * CB, KL), F32),
            pltpu.VMEM((STRIPES, CB * R, KL), BF),
            pltpu.VMEM((SLOTS, 4 * CB, QW), BF),
            dma, dma((NC,)), dma((NC,)), dma((NC,)), dma((NC,)), dma((NC,)), dma((NC,)),
            dma((NG,)), dma((NG,)), dma((NG,)), dma((NG,)), dma((2, 4)), dma((2, 4)),
        ],
        compiler_params=pltpu.CompilerParams(
            collective_id=0, has_side_effects=True, vmem_limit_bytes=56 << 20
        ),
        cost_estimate=pl.CostEstimate(flops=12 << 30, bytes_accessed=8 << 20, transcendentals=0),
    )(raw_strain, whitening_taps, first_block, pair_owner.reshape(PAIRS))
    return pl.pallas_call(
        finish,
        grid=(SLOTS,),
        out_shape=jax.ShapeDtypeStruct((SLOTS, CB, CB, LAGS), F32),
        in_specs=[pl.BlockSpec((1, 256, 256), lambda s: (s, 0, 0))],
        out_specs=pl.BlockSpec((1, CB, CB, LAGS), lambda s: (s, 0, 0, 0)),
    )(acc)


def solution(mesh):
    in_specs = (P(("tgroup", "chan"), None), P(), P("chan"), P("chan", None))
    out_specs = P(("tgroup", "chan"), None, None, None)
    return jax.shard_map(local, mesh=mesh, in_specs=in_specs, out_specs=out_specs, check_vma=False)
```

```python
import math

import jax
import jax.numpy as jnp
from jax import lax
from jax.experimental import pallas as pl
from jax.experimental.pallas import tpu as pltpu
from jax.sharding import PartitionSpec as P

MESH = pl.DeviceIdType.MESH
MAXLAG = 500
LAGS = 1001
CB = 8
K = 8
STRIPES = 2
SLOTS = 5
TAPS = 255
NG = 8
NC = 32
CPD = 320
CHANNELS = 10240
ROWS = 128
TS = 4096
TD = 2048
HALF = TD // 2
PAIRS = STRIPES * K
WIDE = CHANNELS + 128
SPAN = 512
EARLY = 80
PACK = 4
AHEAD = 2
IN_FLIGHT = 4
FB = 256
FW = 768
R = 32
KL = TD + 128
QW = TD + 1024
F32 = jnp.float32
BF = jnp.bfloat16
I32 = jnp.int32


def remote(src, dst, send_sem, recv_sem, axis, target):
    return pltpu.make_async_remote_copy(
        src_ref=src, dst_ref=dst, send_sem=send_sem, recv_sem=recv_sem,
        device_id={axis: target}, device_id_type=MESH,
    )


def kernel(
    raw_ref, taps_ref, fb_ref, owner_ref, acc,
    raw_v, raw_b, table_v, mine_v, send_v, x_v, filt, send0, recv0, send1, recv1, leads, lead_f, shifted, windows,
    raw_sem, fsend, frecv, asend, arecv, bsend, brecv, s0, r0, s1, r1, ls, lr,
):
    me_c = lax.axis_index("chan")
    me_g = lax.axis_index("tgroup")

    barrier = pltpu.get_barrier_semaphore()

    def greet_chan(d, carry):
        pl.semaphore_signal(barrier, inc=1, device_id={"chan": lax.rem(me_c + d, NC)}, device_id_type=MESH)
        return carry

    def greet_group(d, carry):
        pl.semaphore_signal(barrier, inc=1, device_id={"tgroup": lax.rem(me_g + d, NG)}, device_id_type=MESH)
        return carry

    lax.fori_loop(1, NC, greet_chan, 0)
    lax.fori_loop(1, NG, greet_group, 0)
    raw_in = pltpu.make_async_copy(raw_ref, raw_v, raw_sem)
    raw_in.start()

    owners = [owner_ref[q] for q in range(PAIRS)]
    slots = []
    for q in range(PAIRS):
        count = jnp.int32(0)
        for earlier in range(q):
            count = count + jnp.where(owners[earlier] == owners[q], 1, 0)
        slots.append(count)
    keys = [jnp.int32(q // K - 2) if q % K == 0 else slots[q] * PAIRS + q for q in range(PAIRS)]
    places = [jnp.int32(0)] * PAIRS
    for q in range(PAIRS):
        for other in range(q):
            ahead = jnp.where(keys[other] < keys[q], 1, 0)
            places[q] = places[q] + ahead
            places[other] = places[other] + 1 - ahead
    place_row = lax.broadcasted_iota(I32, (PAIRS, 128), 0)
    place_lane = lax.broadcasted_iota(I32, (1, 128), 1) // CB
    starts = jnp.zeros((PAIRS, 128), I32)
    target = jnp.zeros((1, 128), I32)
    for q in range(PAIRS):
        starts = jnp.where(place_row == places[q], (fb_ref[q // K] + q % K) * CB, starts)
        target = jnp.where(place_lane == places[q], owners[q] * SLOTS + slots[q], target)
    mine_v[...] = starts
    table_v[me_c] = starts
    stripe_of = []
    for s in range(SLOTS):
        value = jnp.int32(0)
        for q in range(K, PAIRS):
            value = value + jnp.where((owners[q] == me_g) & (slots[q] == s), 1, 0)
        stripe_of.append(value)

    raw_b[:, pl.ds(CHANNELS, 128)] = jnp.zeros((ROWS, 128), BF)
    x_v[0] = jnp.zeros((128, ROWS), BF)
    x_v[NC + 1] = jnp.zeros((128, ROWS), BF)
    lead_f[:, pl.ds(TD, 128)] = jnp.zeros((STRIPES * CB, 128), F32)

    pl.semaphore_wait(barrier, NC + NG - 2)

    def first_copy(d, peer, owner):
        return remote(mine_v, table_v.at[owner], fsend.at[d], frecv.at[d], "chan", peer)

    def send_first(d, carry):
        first_copy(d, lax.rem(me_c + d, NC), me_c).start()
        return carry

    lax.fori_loop(1, NC, send_first, 0)

    line = jnp.concatenate([taps_ref[...].reshape(1, TAPS), jnp.zeros((1, FW - TAPS), F32)], 1)
    band = pltpu.roll(jnp.broadcast_to(line, (FB, FW)), 1, 1, stride=2, stride_axis=0)
    band_hi = band.astype(BF)
    band_lo = (band - band_hi.astype(F32)).astype(BF)

    raw_in.wait()

    def round_raw(i, carry):
        at = pl.multiple_of(i * 512, 512)
        raw_b[:, pl.ds(at, 512)] = raw_v[:, pl.ds(at, 512)].astype(BF)
        return carry

    lax.fori_loop(0, CHANNELS // 512, round_raw, 0)

    def wait_first(d, carry):
        peer = lax.rem(me_c + NC - d, NC)
        first_copy(d, peer, peer).wait_recv()
        return carry

    lax.fori_loop(1, NC, wait_first, 0)

    ahead_by = lax.broadcasted_iota(I32, (CB, SPAN), 1) - lax.broadcasted_iota(I32, (CB, SPAN), 0)

    def packed(dst):
        base = (dst * CPD) // 128 * 128
        shift = dst * CPD - base
        hot = []
        for place in range(PAIRS):
            wanted = jnp.broadcast_to(table_v[dst, pl.ds(place, 1), :] + shift, (CB, 128))
            hot.append(jnp.where(ahead_by == jnp.concatenate([wanted] * (SPAN // 128), 1), 1.0, 0.0))
        chosen = jnp.concatenate(hot, 0).astype(BF)
        source = raw_b[:, pl.ds(pl.multiple_of(base, 128), SPAN)]
        return lax.dot_general(chosen, source, (((1,), (1,)), ((), ())), preferred_element_type=F32).astype(BF)

    def early_copy(d, dst, src):
        return remote(
            send_v.at[dst, pl.ds(0, EARLY)], x_v.at[1 + src, pl.ds(0, EARLY)], asend.at[d], arecv.at[d], "chan", dst
        )

    def late_copy(d, dst, src):
        return remote(
            send_v.at[dst, pl.ds(EARLY, 128 - EARLY)], x_v.at[1 + src, pl.ds(EARLY, 128 - EARLY)],
            bsend.at[d], brecv.at[d], "chan", dst,
        )

    def send_early(i, carry):
        dsts = [lax.rem(me_c + i * PACK + j, NC) for j in range(PACK)]
        for dst, part in zip(dsts, [packed(dst) for dst in dsts]):
            send_v[dst] = part
        for j, dst in enumerate(dsts):

            @pl.when(i * PACK + j > 0)
            def _():
                early_copy(i * PACK + j, dst, me_c).start()

        return carry

    def send_late(d, carry):
        late_copy(d, lax.rem(me_c + d, NC), me_c).start()
        return carry

    lax.fori_loop(0, NC // PACK, send_early, 0)
    lax.fori_loop(1, NC, send_late, 0)
    x_v[1 + me_c] = send_v[me_c]

    def wait_early(d, carry):
        peer = lax.rem(me_c + NC - d, NC)
        early_copy(d, peer, peer).wait_recv()
        return carry

    def wait_late(d, carry):
        peer = lax.rem(me_c + NC - d, NC)
        late_copy(d, peer, peer).wait_recv()
        return carry

    def whiten(at, count):
        window = jnp.concatenate(
            [
                jnp.concatenate([x_v[4 * block + part, pl.ds(at, count)] for part in range(FW // ROWS)], 1)
                for block in range(TD // FB)
            ],
            0,
        )
        y = sum(
            lax.dot_general(window, term, (((1,), (1,)), ((), ())), preferred_element_type=F32)
            for term in (band_hi, band_lo)
        )
        for block in range(TD // FB):
            filt[pl.ds(at, count), pl.ds(block * FB, FB)] = y[block * count:(block + 1) * count].astype(BF)

    def chosen_rows(first, count, depth):
        rows = NG * count * CB
        row_id = lax.broadcasted_iota(I32, (rows, depth), 0)
        col_id = lax.broadcasted_iota(I32, (rows, depth), 1)
        wanted = row_id // (count * CB) * SLOTS + first + row_id // CB % count
        pick = (jnp.broadcast_to(target[:, :depth], (rows, depth)) == wanted) & (row_id % CB == col_id % CB)
        rows_of = jnp.dot(
            jnp.where(pick, 1.0, 0.0).astype(BF), filt[pl.ds(0, depth)], preferred_element_type=F32
        )
        parts = [rows_of[o * count * CB:(o + 1) * count * CB] for o in range(NG)]
        return [jnp.concatenate([part[:, :HALF], part[:, HALF:]], 0).astype(BF) for part in parts]

    lax.fori_loop(1, NC, wait_early, 0)
    whiten(0, EARLY)

    right = lax.rem(me_g + 1, NG)
    left = lax.rem(me_g + NG - 1, NG)

    def lead_copy(way, hop):
        back = hop - 1 if way == 0 else NG - hop + 1
        origin = lax.rem(me_g + NG - back, NG)
        part = leads.at[origin] if hop < 4 else leads.at[origin, way]
        return remote(part, part, ls.at[way, hop - 1], lr.at[way, hop - 1], "tgroup", right if way == 0 else left)

    def lead_arrival(way, hop):
        back = hop if way == 0 else NG - hop
        origin = lax.rem(me_g + NG - back, NG)
        part = leads.at[origin] if hop < 4 else leads.at[origin, way]
        return remote(part, part, ls.at[way, hop - 1], lr.at[way, hop - 1], "tgroup", right if way == 0 else left)

    def pass_leads(hop):
        for way in range(2):
            lead_arrival(way, hop - 1).wait_recv()
            lead_copy(way, hop).start()

    for half in range(2):
        leads[me_g, half] = filt[pl.ds(0, STRIPES * CB), pl.ds(half * HALF, HALF)]
    for way in range(2):
        lead_copy(way, 1).start()

    def step_offset(i):
        return jnp.where(i % 2 == 1, (i + 1) // 2, NG - i // 2)

    def slot0_copy(i, dst, src):
        return remote(send0.at[dst], recv0.at[src], s0.at[i], r0.at[i], "tgroup", dst)

    def slot1_copy(i, dst, src):
        return remote(send1.at[dst], recv1.at[src], s1.at[i], r1.at[i], "tgroup", dst)

    def send_slot0(i, carry):
        slot0_copy(i, lax.rem(me_g + step_offset(i), NG), me_g).start()
        return carry

    def send_slot1(i, carry):
        slot1_copy(i, lax.rem(me_g + step_offset(i), NG), me_g).start()
        return carry

    for owner, part in enumerate(chosen_rows(0, 1, EARLY)):
        send0[owner] = part
    lax.fori_loop(1, NG, send_slot0, 0)
    recv0[me_g] = send0[me_g]

    def spread_leads(src):
        for half in range(2):
            lead_f[:, pl.ds(half * HALF, HALF)] = leads[src, half].astype(F32)
        for row in range(STRIPES * CB):
            line = jnp.broadcast_to(lead_f[pl.ds(row, 1)], (R, KL))
            turned = pltpu.roll(line, 0, 1, stride=1, stride_axis=0)
            shifted[src, row // CB, pl.ds(row % CB * R, R)] = turned.astype(BF)

    def correlate(src, halves, first, count, fresh=False):
        width = count * CB
        halves = halves.astype(F32)
        padded = jnp.concatenate([halves[:width], halves[width:], jnp.zeros((width, QW - TD), F32)], 1)
        turns = [pltpu.roll(padded, MAXLAG - R * step, 1) for step in range(128 // R)]
        for s in range(count):
            windows[first + s] = jnp.concatenate([turn[s * CB:(s + 1) * CB] for turn in turns], 0).astype(BF)
        for slot in range(first, first + count):
            partner = jnp.concatenate(
                [windows[slot, :, pl.ds(128 * step, KL)] for step in range(1024 // 128)], 0
            )
            product = lax.dot_general(
                partner, shifted[src, stripe_of[slot]], (((1,), (1,)), ((), ())), preferred_element_type=F32
            )
            acc[slot] = product if fresh else acc[slot] + product

    spread_leads(me_g)
    correlate(me_g, recv0[me_g], 0, 1, True)
    pass_leads(2)

    def source(i):
        return lax.rem(me_g + NG - step_offset(i), NG)

    def first_pass(i):
        src = source(i)
        spread_leads(src)
        slot0_copy(i, src, src).wait_recv()
        correlate(src, recv0[src], 0, 1)

    def ahead(i, carry):
        first_pass(i)
        return carry

    lax.fori_loop(1, 1 + AHEAD, ahead, 0)

    lax.fori_loop(1, NC, wait_late, 0)
    whiten(EARLY, 128 - EARLY)
    for owner, part in enumerate(chosen_rows(1, SLOTS - 1, 128)):
        send1[owner] = part
    lax.fori_loop(1, 3, send_slot1, 0)
    pass_leads(3)
    lax.fori_loop(3, 1 + IN_FLIGHT, send_slot1, 0)
    correlate(me_g, send1[me_g], 1, SLOTS - 1, True)

    def receive(i, carry):
        @pl.when(i + AHEAD == 5)
        def _():
            pass_leads(4)

        @pl.when(i + AHEAD == NG - 1)
        def _():
            for way in range(2):
                lead_arrival(way, 4).wait_recv()

        @pl.when(i + AHEAD < NG)
        def _():
            first_pass(i + AHEAD)

        src = source(i)
        slot1_copy(i, src, src).wait_recv()

        @pl.when(i + IN_FLIGHT < NG)
        def _():
            send_slot1(i + IN_FLIGHT, 0)

        correlate(src, recv1[src], 1, SLOTS - 1)
        return carry

    lax.fori_loop(1, NG, receive, 0)

    def wait_chan_sent(d, carry):
        dst = lax.rem(me_c + d, NC)
        first_copy(d, dst, me_c).wait_send()
        early_copy(d, dst, me_c).wait_send()
        late_copy(d, dst, me_c).wait_send()
        return carry

    lax.fori_loop(1, NC, wait_chan_sent, 0)

    def wait_group_sent(i, carry):
        dst = lax.rem(me_g + step_offset(i), NG)
        slot0_copy(i, dst, me_g).wait_send()
        slot1_copy(i, dst, me_g).wait_send()
        return carry

    lax.fori_loop(1, NG, wait_group_sent, 0)
    for way in range(2):
        for hop in range(1, 5):
            lead_copy(way, hop).wait_send()


def finish(acc_ref, out_ref, acc_v, out_v, in_sem, out_sem):
    scale = 1.0 / math.sqrt(TD)
    lane = lax.broadcasted_iota(I32, (CB, 128), 1)
    low, even = lane < 64, lane // R % 2 == 0

    def fetch(slot):
        return pltpu.make_async_copy(acc_ref.at[slot], acc_v.at[slot], in_sem.at[slot])

    def put(slot):
        return pltpu.make_async_copy(out_v.at[slot], out_ref.at[slot], out_sem.at[slot])

    for slot in range(SLOTS):
        fetch(slot).start()

    def one_slot(slot, carry):
        fetch(slot).wait()
        for step in range(1024 // 128):
            for half in range(2):
                p = [
                    acc_v[slot, pl.ds(step * 4 * CB + s * CB, CB), pl.ds(half * 128, 128)] * scale for s in range(4)
                ]
                far = [None] * 4
                for s in range(2):
                    far[s] = jnp.where(low, p[s], pltpu.roll(p[s + 2], 64, 1))
                    far[s + 2] = jnp.where(low, pltpu.roll(p[s], 64, 1), p[s + 2])
                width = min(128, LAGS - step * 128)
                for s in (0, 2):
                    first = jnp.where(even, far[s], pltpu.roll(far[s + 1], R, 1))
                    second = jnp.where(even, pltpu.roll(far[s], 128 - R, 1), far[s + 1])
                    out_v[slot, half * 4 + s, :, pl.ds(step * 128, width)] = first[:, :width]
                    out_v[slot, half * 4 + s + 1, :, pl.ds(step * 128, width)] = second[:, :width]
        put(slot).start()
        return carry

    lax.fori_loop(0, SLOTS, one_slot, 0)
    for slot in range(SLOTS):
        put(slot).wait()


def local(raw_strain, whitening_taps, first_block, pair_owner):
    vmem = pl.BlockSpec(memory_space=pltpu.VMEM)
    smem = pl.BlockSpec(memory_space=pltpu.SMEM)
    dma = pltpu.SemaphoreType.DMA
    acc = pl.pallas_call(
        kernel,
        out_shape=jax.ShapeDtypeStruct((SLOTS, 256, 256), F32),
        in_specs=[pl.BlockSpec(memory_space=pl.ANY), vmem, smem, smem],
        out_specs=vmem,
        scratch_shapes=[
            pltpu.VMEM((ROWS, CHANNELS), F32),
            pltpu.VMEM((ROWS, WIDE), BF),
            pltpu.VMEM((NC, PAIRS, 128), I32),
            pltpu.VMEM((PAIRS, 128), I32),
            pltpu.VMEM((NC, 128, ROWS), BF),
            pltpu.VMEM((NC + 2, 128, ROWS), BF),
            pltpu.VMEM((128, TD), BF),
            pltpu.VMEM((NG, 2 * CB, HALF), BF),
            pltpu.VMEM((NG, 2 * CB, HALF), BF),
            pltpu.VMEM((NG, 2 * CB * (SLOTS - 1), HALF), BF),
            pltpu.VMEM((NG, 2 * CB * (SLOTS - 1), HALF), BF),
            pltpu.VMEM((NG, 2, STRIPES * CB, HALF), BF),
            pltpu.VMEM((STRIPES * CB, KL), F32),
            pltpu.VMEM((NG, STRIPES, CB * R, KL), BF),
            pltpu.VMEM((SLOTS, 4 * CB, QW), BF),
            dma, dma((NC,)), dma((NC,)), dma((NC,)), dma((NC,)), dma((NC,)), dma((NC,)),
            dma((NG,)), dma((NG,)), dma((NG,)), dma((NG,)), dma((2, 4)), dma((2, 4)),
        ],
        compiler_params=pltpu.CompilerParams(
            collective_id=0, has_side_effects=True, vmem_limit_bytes=56 << 20
        ),
        cost_estimate=pl.CostEstimate(flops=12 << 30, bytes_accessed=8 << 20, transcendentals=0),
    )(raw_strain, whitening_taps, first_block, pair_owner.reshape(PAIRS))
    return pl.pallas_call(
        finish,
        out_shape=jax.ShapeDtypeStruct((SLOTS, CB, CB, LAGS), F32),
        in_specs=[pl.BlockSpec(memory_space=pltpu.HBM)],
        out_specs=pl.BlockSpec(memory_space=pltpu.HBM),
        scratch_shapes=[
            pltpu.VMEM((SLOTS, 256, 256), F32), pltpu.VMEM((SLOTS, CB, CB, LAGS), F32), dma((SLOTS,)), dma((SLOTS,)),
        ],
    )(acc)


def solution(mesh):
    in_specs = (P(("tgroup", "chan"), None), P(), P("chan"), P("chan", None))
    out_specs = P(("tgroup", "chan"), None, None, None)
    return jax.shard_map(local, mesh=mesh, in_specs=in_specs, out_specs=out_specs, check_vma=False)
```

```python
import math

import jax
import jax.numpy as jnp
from jax import lax
from jax.experimental import pallas as pl
from jax.experimental.pallas import tpu as pltpu
from jax.sharding import PartitionSpec as P

MESH = pl.DeviceIdType.MESH
MAXLAG = 500
LAGS = 1001
CB = 8
K = 8
STRIPES = 2
SLOTS = 5
TAPS = 255
NG = 8
NC = 32
CPD = 320
CHANNELS = 10240
ROWS = 128
TS = 4096
TD = 2048
HALF = TD // 2
PAIRS = STRIPES * K
WIDE = CHANNELS + 128
SPAN = 512
EARLY = 80
PACK = 4
AHEAD = 2
IN_FLIGHT = 4
FB = 256
FW = 768
R = 32
KL = TD + 128
QW = TD + 1024
F32 = jnp.float32
BF = jnp.bfloat16
I32 = jnp.int32


def remote(src, dst, send_sem, recv_sem, axis, target):
    return pltpu.make_async_remote_copy(
        src_ref=src, dst_ref=dst, send_sem=send_sem, recv_sem=recv_sem,
        device_id={axis: target}, device_id_type=MESH,
    )


def kernel(
    raw_ref, taps_ref, fb_ref, owner_ref, acc,
    raw_v, raw_b, table_v, mine_v, send_v, x_v, filt, send0, recv0, send1, recv1, leads, lead_f, shifted, windows,
    raw_sem, fsend, frecv, asend, arecv, bsend, brecv, s0, r0, s1, r1, ls, lr,
):
    me_c = lax.axis_index("chan")
    me_g = lax.axis_index("tgroup")

    barrier = pltpu.get_barrier_semaphore()

    def greet_chan(d, carry):
        pl.semaphore_signal(barrier, inc=1, device_id={"chan": lax.rem(me_c + d, NC)}, device_id_type=MESH)
        return carry

    def greet_group(d, carry):
        pl.semaphore_signal(barrier, inc=1, device_id={"tgroup": lax.rem(me_g + d, NG)}, device_id_type=MESH)
        return carry

    lax.fori_loop(1, NC, greet_chan, 0)
    lax.fori_loop(1, NG, greet_group, 0)
    raw_in = pltpu.make_async_copy(raw_ref, raw_v, raw_sem)
    raw_in.start()

    owners = [owner_ref[q] for q in range(PAIRS)]
    slots = []
    for q in range(PAIRS):
        count = jnp.int32(0)
        for earlier in range(q):
            count = count + jnp.where(owners[earlier] == owners[q], 1, 0)
        slots.append(count)
    keys = [jnp.int32(q // K - 2) if q % K == 0 else slots[q] * PAIRS + q for q in range(PAIRS)]
    places = [jnp.int32(0)] * PAIRS
    for q in range(PAIRS):
        for other in range(q):
            ahead = jnp.where(keys[other] < keys[q], 1, 0)
            places[q] = places[q] + ahead
            places[other] = places[other] + 1 - ahead
    place_row = lax.broadcasted_iota(I32, (PAIRS, 128), 0)
    place_lane = lax.broadcasted_iota(I32, (1, 128), 1) // CB
    starts = jnp.zeros((PAIRS, 128), I32)
    target = jnp.zeros((1, 128), I32)
    for q in range(PAIRS):
        starts = jnp.where(place_row == places[q], (fb_ref[q // K] + q % K) * CB, starts)
        target = jnp.where(place_lane == places[q], owners[q] * SLOTS + slots[q], target)
    mine_v[...] = starts
    table_v[me_c] = starts
    stripe_of = []
    for s in range(SLOTS):
        value = jnp.int32(0)
        for q in range(K, PAIRS):
            value = value + jnp.where((owners[q] == me_g) & (slots[q] == s), 1, 0)
        stripe_of.append(value)

    raw_b[:, pl.ds(CHANNELS, 128)] = jnp.zeros((ROWS, 128), BF)
    x_v[0] = jnp.zeros((128, ROWS), BF)
    x_v[NC + 1] = jnp.zeros((128, ROWS), BF)
    lead_f[:, pl.ds(TD, 128)] = jnp.zeros((STRIPES * CB, 128), F32)

    pl.semaphore_wait(barrier, NC + NG - 2)

    def first_copy(d, peer, owner):
        return remote(mine_v, table_v.at[owner], fsend.at[d], frecv.at[d], "chan", peer)

    def send_first(d, carry):
        first_copy(d, lax.rem(me_c + d, NC), me_c).start()
        return carry

    lax.fori_loop(1, NC, send_first, 0)

    line = jnp.concatenate([taps_ref[...].reshape(1, TAPS), jnp.zeros((1, FW - TAPS), F32)], 1)
    band = pltpu.roll(jnp.broadcast_to(line, (FB, FW)), 1, 1, stride=2, stride_axis=0)
    band_hi = band.astype(BF)
    band_lo = (band - band_hi.astype(F32)).astype(BF)

    raw_in.wait()

    def round_raw(i, carry):
        at = pl.multiple_of(i * 512, 512)
        raw_b[:, pl.ds(at, 512)] = raw_v[:, pl.ds(at, 512)].astype(BF)
        return carry

    lax.fori_loop(0, CHANNELS // 512, round_raw, 0)

    ahead_by = lax.broadcasted_iota(I32, (CB, SPAN), 1) - lax.broadcasted_iota(I32, (CB, SPAN), 0)

    def packed(dst):
        base = (dst * CPD) // 128 * 128
        shift = dst * CPD - base
        hot = []
        for place in range(PAIRS):
            wanted = jnp.broadcast_to(table_v[dst, pl.ds(place, 1), :] + shift, (CB, 128))
            hot.append(jnp.where(ahead_by == jnp.concatenate([wanted] * (SPAN // 128), 1), 1.0, 0.0))
        chosen = jnp.concatenate(hot, 0).astype(BF)
        source = raw_b[:, pl.ds(pl.multiple_of(base, 128), SPAN)]
        return lax.dot_general(chosen, source, (((1,), (1,)), ((), ())), preferred_element_type=F32).astype(BF)

    def early_copy(d, dst, src):
        return remote(
            send_v.at[dst, pl.ds(0, EARLY)], x_v.at[1 + src, pl.ds(0, EARLY)], asend.at[d], arecv.at[d], "chan", dst
        )

    def late_copy(d, dst, src):
        return remote(
            send_v.at[dst, pl.ds(EARLY, 128 - EARLY)], x_v.at[1 + src, pl.ds(EARLY, 128 - EARLY)],
            bsend.at[d], brecv.at[d], "chan", dst,
        )

    def send_early(i, carry):
        dsts = [lax.rem(me_c + NC - i * PACK - j, NC) for j in range(PACK)]
        for j, dst in enumerate(dsts):

            @pl.when(i * PACK + j > 0)
            def _():
                first_copy(i * PACK + j, dst, dst).wait_recv()

        for dst, part in zip(dsts, [packed(dst) for dst in dsts]):
            send_v[dst] = part
        for j, dst in enumerate(dsts):

            @pl.when(i * PACK + j > 0)
            def _():
                early_copy(i * PACK + j, dst, me_c).start()

        return carry

    def send_late(d, carry):
        late_copy(d, lax.rem(me_c + NC - d, NC), me_c).start()
        return carry

    lax.fori_loop(0, NC // PACK, send_early, 0)
    lax.fori_loop(1, NC, send_late, 0)
    x_v[1 + me_c] = send_v[me_c]

    def wait_early(d, carry):
        peer = lax.rem(me_c + d, NC)
        early_copy(d, peer, peer).wait_recv()
        return carry

    def wait_late(d, carry):
        peer = lax.rem(me_c + d, NC)
        late_copy(d, peer, peer).wait_recv()
        return carry

    def whiten(at, count):
        window = jnp.concatenate(
            [
                jnp.concatenate([x_v[4 * block + part, pl.ds(at, count)] for part in range(FW // ROWS)], 1)
                for block in range(TD // FB)
            ],
            0,
        )
        y = sum(
            lax.dot_general(window, term, (((1,), (1,)), ((), ())), preferred_element_type=F32)
            for term in (band_hi, band_lo)
        )
        for block in range(TD // FB):
            filt[pl.ds(at, count), pl.ds(block * FB, FB)] = y[block * count:(block + 1) * count].astype(BF)

    def chosen_rows(first, count, depth):
        rows = NG * count * CB
        row_id = lax.broadcasted_iota(I32, (rows, depth), 0)
        col_id = lax.broadcasted_iota(I32, (rows, depth), 1)
        wanted = row_id // (count * CB) * SLOTS + first + row_id // CB % count
        pick = (jnp.broadcast_to(target[:, :depth], (rows, depth)) == wanted) & (row_id % CB == col_id % CB)
        rows_of = jnp.dot(
            jnp.where(pick, 1.0, 0.0).astype(BF), filt[pl.ds(0, depth)], preferred_element_type=F32
        )
        parts = [rows_of[o * count * CB:(o + 1) * count * CB] for o in range(NG)]
        return [jnp.concatenate([part[:, :HALF], part[:, HALF:]], 0).astype(BF) for part in parts]

    lax.fori_loop(1, NC, wait_early, 0)
    whiten(0, EARLY)

    right = lax.rem(me_g + 1, NG)
    left = lax.rem(me_g + NG - 1, NG)

    def lead_copy(way, hop):
        back = hop - 1 if way == 0 else NG - hop + 1
        origin = lax.rem(me_g + NG - back, NG)
        part = leads.at[origin] if hop < 4 else leads.at[origin, way]
        return remote(part, part, ls.at[way, hop - 1], lr.at[way, hop - 1], "tgroup", right if way == 0 else left)

    def lead_arrival(way, hop):
        back = hop if way == 0 else NG - hop
        origin = lax.rem(me_g + NG - back, NG)
        part = leads.at[origin] if hop < 4 else leads.at[origin, way]
        return remote(part, part, ls.at[way, hop - 1], lr.at[way, hop - 1], "tgroup", right if way == 0 else left)

    def pass_leads(hop):
        for way in range(2):
            lead_arrival(way, hop - 1).wait_recv()
            lead_copy(way, hop).start()

    for half in range(2):
        leads[me_g, half] = filt[pl.ds(0, STRIPES * CB), pl.ds(half * HALF, HALF)]
    for way in range(2):
        lead_copy(way, 1).start()

    def step_offset(i):
        return jnp.where(i % 2 == 1, (i + 1) // 2, NG - i // 2)

    def slot0_copy(i, dst, src):
        return remote(send0.at[dst], recv0.at[src], s0.at[i], r0.at[i], "tgroup", dst)

    def slot1_copy(i, dst, src):
        return remote(send1.at[dst], recv1.at[src], s1.at[i], r1.at[i], "tgroup", dst)

    def send_slot0(i, carry):
        slot0_copy(i, lax.rem(me_g + step_offset(i), NG), me_g).start()
        return carry

    def send_slot1(i, carry):
        slot1_copy(i, lax.rem(me_g + step_offset(i), NG), me_g).start()
        return carry

    for owner, part in enumerate(chosen_rows(0, 1, EARLY)):
        send0[owner] = part
    lax.fori_loop(1, NG, send_slot0, 0)
    recv0[me_g] = send0[me_g]

    def spread_leads(src):
        for half in range(2):
            lead_f[:, pl.ds(half * HALF, HALF)] = leads[src, half].astype(F32)
        for row in range(STRIPES * CB):
            line = jnp.broadcast_to(lead_f[pl.ds(row, 1)], (R, KL))
            turned = pltpu.roll(line, 0, 1, stride=1, stride_axis=0)
            shifted[src, row // CB, pl.ds(row % CB * R, R)] = turned.astype(BF)

    def correlate(src, halves, first, count, fresh=False):
        width = count * CB
        halves = halves.astype(F32)
        padded = jnp.concatenate([halves[:width], halves[width:], jnp.zeros((width, QW - TD), F32)], 1)
        turns = [pltpu.roll(padded, MAXLAG - R * step, 1) for step in range(128 // R)]
        for s in range(count):
            windows[first + s] = jnp.concatenate([turn[s * CB:(s + 1) * CB] for turn in turns], 0).astype(BF)
        for slot in range(first, first + count):
            partner = jnp.concatenate(
                [windows[slot, :, pl.ds(128 * step, KL)] for step in range(1024 // 128)], 0
            )
            product = lax.dot_general(
                partner, shifted[src, stripe_of[slot]], (((1,), (1,)), ((), ())), preferred_element_type=F32
            )
            acc[slot] = product if fresh else acc[slot] + product

    spread_leads(me_g)
    correlate(me_g, recv0[me_g], 0, 1, True)
    pass_leads(2)

    def source(i):
        return lax.rem(me_g + NG - step_offset(i), NG)

    def first_pass(i):
        src = source(i)
        spread_leads(src)
        slot0_copy(i, src, src).wait_recv()
        correlate(src, recv0[src], 0, 1)

    def ahead(i, carry):
        first_pass(i)
        return carry

    lax.fori_loop(1, 1 + AHEAD, ahead, 0)

    lax.fori_loop(1, NC, wait_late, 0)
    whiten(EARLY, 128 - EARLY)
    for owner, part in enumerate(chosen_rows(1, SLOTS - 1, 128)):
        send1[owner] = part
    lax.fori_loop(1, 3, send_slot1, 0)
    pass_leads(3)
    lax.fori_loop(3, 1 + IN_FLIGHT, send_slot1, 0)
    correlate(me_g, send1[me_g], 1, SLOTS - 1, True)

    def receive(i, carry):
        @pl.when(i + AHEAD == 5)
        def _():
            pass_leads(4)

        @pl.when(i + AHEAD == NG - 1)
        def _():
            for way in range(2):
                lead_arrival(way, 4).wait_recv()

        @pl.when(i + AHEAD < NG)
        def _():
            first_pass(i + AHEAD)

        src = source(i)
        slot1_copy(i, src, src).wait_recv()

        @pl.when(i + IN_FLIGHT < NG)
        def _():
            send_slot1(i + IN_FLIGHT, 0)

        correlate(src, recv1[src], 1, SLOTS - 1)
        return carry

    lax.fori_loop(1, NG, receive, 0)

    def wait_chan_sent(d, carry):
        dst, back = lax.rem(me_c + d, NC), lax.rem(me_c + NC - d, NC)
        first_copy(d, dst, me_c).wait_send()
        early_copy(d, back, me_c).wait_send()
        late_copy(d, back, me_c).wait_send()
        return carry

    lax.fori_loop(1, NC, wait_chan_sent, 0)

    def wait_group_sent(i, carry):
        dst = lax.rem(me_g + step_offset(i), NG)
        slot0_copy(i, dst, me_g).wait_send()
        slot1_copy(i, dst, me_g).wait_send()
        return carry

    lax.fori_loop(1, NG, wait_group_sent, 0)
    for way in range(2):
        for hop in range(1, 5):
            lead_copy(way, hop).wait_send()


def finish(acc_ref, out_ref, acc_v, out_v, in_sem, out_sem):
    scale = 1.0 / math.sqrt(TD)
    lane = lax.broadcasted_iota(I32, (CB, 128), 1)
    low, even = lane < 64, lane // R % 2 == 0

    def fetch(slot):
        return pltpu.make_async_copy(acc_ref.at[slot], acc_v.at[slot], in_sem.at[slot])

    def put(slot):
        return pltpu.make_async_copy(out_v.at[slot], out_ref.at[slot], out_sem.at[slot])

    for slot in range(SLOTS):
        fetch(slot).start()

    def one_slot(slot, carry):
        fetch(slot).wait()
        for step in range(1024 // 128):
            for half in range(2):
                p = [
                    acc_v[slot, pl.ds(step * 4 * CB + s * CB, CB), pl.ds(half * 128, 128)] * scale for s in range(4)
                ]
                far = [None] * 4
                for s in range(2):
                    far[s] = jnp.where(low, p[s], pltpu.roll(p[s + 2], 64, 1))
                    far[s + 2] = jnp.where(low, pltpu.roll(p[s], 64, 1), p[s + 2])
                width = min(128, LAGS - step * 128)
                for s in (0, 2):
                    first = jnp.where(even, far[s], pltpu.roll(far[s + 1], R, 1))
                    second = jnp.where(even, pltpu.roll(far[s], 128 - R, 1), far[s + 1])
                    out_v[slot, half * 4 + s, :, pl.ds(step * 128, width)] = first[:, :width]
                    out_v[slot, half * 4 + s + 1, :, pl.ds(step * 128, width)] = second[:, :width]
        put(slot).start()
        return carry

    lax.fori_loop(0, SLOTS, one_slot, 0)
    for slot in range(SLOTS):
        put(slot).wait()


def local(raw_strain, whitening_taps, first_block, pair_owner):
    vmem = pl.BlockSpec(memory_space=pltpu.VMEM)
    smem = pl.BlockSpec(memory_space=pltpu.SMEM)
    dma = pltpu.SemaphoreType.DMA
    acc = pl.pallas_call(
        kernel,
        out_shape=jax.ShapeDtypeStruct((SLOTS, 256, 256), F32),
        in_specs=[pl.BlockSpec(memory_space=pl.ANY), vmem, smem, smem],
        out_specs=vmem,
        scratch_shapes=[
            pltpu.VMEM((ROWS, CHANNELS), F32),
            pltpu.VMEM((ROWS, WIDE), BF),
            pltpu.VMEM((NC, PAIRS, 128), I32),
            pltpu.VMEM((PAIRS, 128), I32),
            pltpu.VMEM((NC, 128, ROWS), BF),
            pltpu.VMEM((NC + 2, 128, ROWS), BF),
            pltpu.VMEM((128, TD), BF),
            pltpu.VMEM((NG, 2 * CB, HALF), BF),
            pltpu.VMEM((NG, 2 * CB, HALF), BF),
            pltpu.VMEM((NG, 2 * CB * (SLOTS - 1), HALF), BF),
            pltpu.VMEM((NG, 2 * CB * (SLOTS - 1), HALF), BF),
            pltpu.VMEM((NG, 2, STRIPES * CB, HALF), BF),
            pltpu.VMEM((STRIPES * CB, KL), F32),
            pltpu.VMEM((NG, STRIPES, CB * R, KL), BF),
            pltpu.VMEM((SLOTS, 4 * CB, QW), BF),
            dma, dma((NC,)), dma((NC,)), dma((NC,)), dma((NC,)), dma((NC,)), dma((NC,)),
            dma((NG,)), dma((NG,)), dma((NG,)), dma((NG,)), dma((2, 4)), dma((2, 4)),
        ],
        compiler_params=pltpu.CompilerParams(
            collective_id=0, has_side_effects=True, vmem_limit_bytes=56 << 20
        ),
        cost_estimate=pl.CostEstimate(flops=12 << 30, bytes_accessed=8 << 20, transcendentals=0),
    )(raw_strain, whitening_taps, first_block, pair_owner.reshape(PAIRS))
    return pl.pallas_call(
        finish,
        out_shape=jax.ShapeDtypeStruct((SLOTS, CB, CB, LAGS), F32),
        in_specs=[pl.BlockSpec(memory_space=pltpu.HBM)],
        out_specs=pl.BlockSpec(memory_space=pltpu.HBM),
        scratch_shapes=[
            pltpu.VMEM((SLOTS, 256, 256), F32), pltpu.VMEM((SLOTS, CB, CB, LAGS), F32), dma((SLOTS,)), dma((SLOTS,)),
        ],
    )(acc)


def solution(mesh):
    in_specs = (P(("tgroup", "chan"), None), P(), P("chan"), P("chan", None))
    out_specs = P(("tgroup", "chan"), None, None, None)
    return jax.shard_map(local, mesh=mesh, in_specs=in_specs, out_specs=out_specs, check_vma=False)
```

```python
import math

import jax
import jax.numpy as jnp
from jax import lax
from jax.experimental import pallas as pl
from jax.experimental.pallas import tpu as pltpu
from jax.sharding import PartitionSpec as P

MESH = pl.DeviceIdType.MESH
MAXLAG = 500
LAGS = 1001
CB = 8
K = 8
STRIPES = 2
SLOTS = 5
TAPS = 255
NG = 8
NC = 32
CPD = 320
CHANNELS = 10240
ROWS = 128
TS = 4096
TD = 2048
HALF = TD // 2
PAIRS = STRIPES * K
WIDE = CHANNELS + 128
SPAN = 512
EARLY = 80
PACK = 8
AHEAD = 2
IN_FLIGHT = 4
FB = 256
FW = 768
R = 32
KL = TD + 128
QW = TD + 1024
F32 = jnp.float32
BF = jnp.bfloat16
I32 = jnp.int32


def remote(src, dst, send_sem, recv_sem, axis, target):
    return pltpu.make_async_remote_copy(
        src_ref=src, dst_ref=dst, send_sem=send_sem, recv_sem=recv_sem,
        device_id={axis: target}, device_id_type=MESH,
    )


def kernel(
    raw_ref, taps_ref, fb_ref, owner_ref, acc,
    raw_v, raw_b, table_v, mine_v, send_v, x_v, filt, send0, recv0, send1, recv1, leads, lead_f, shifted, windows,
    raw_sem, fsend, frecv, asend, arecv, bsend, brecv, s0, r0, s1, r1, ls, lr,
):
    me_c = lax.axis_index("chan")
    me_g = lax.axis_index("tgroup")

    barrier = pltpu.get_barrier_semaphore()

    def greet_chan(d, carry):
        pl.semaphore_signal(barrier, inc=1, device_id={"chan": lax.rem(me_c + d, NC)}, device_id_type=MESH)
        return carry

    def greet_group(d, carry):
        pl.semaphore_signal(barrier, inc=1, device_id={"tgroup": lax.rem(me_g + d, NG)}, device_id_type=MESH)
        return carry

    lax.fori_loop(1, NC, greet_chan, 0)
    lax.fori_loop(1, NG, greet_group, 0)
    raw_in = pltpu.make_async_copy(raw_ref, raw_v, raw_sem)
    raw_in.start()

    owners = [owner_ref[q] for q in range(PAIRS)]
    slots = []
    for q in range(PAIRS):
        count = jnp.int32(0)
        for earlier in range(q):
            count = count + jnp.where(owners[earlier] == owners[q], 1, 0)
        slots.append(count)
    keys = [jnp.int32(q // K - 2) if q % K == 0 else slots[q] * PAIRS + q for q in range(PAIRS)]
    places = [jnp.int32(0)] * PAIRS
    for q in range(PAIRS):
        for other in range(q):
            ahead = jnp.where(keys[other] < keys[q], 1, 0)
            places[q] = places[q] + ahead
            places[other] = places[other] + 1 - ahead
    place_row = lax.broadcasted_iota(I32, (PAIRS, 128), 0)
    place_lane = lax.broadcasted_iota(I32, (1, 128), 1) // CB
    starts = jnp.zeros((PAIRS, 128), I32)
    target = jnp.zeros((1, 128), I32)
    for q in range(PAIRS):
        starts = jnp.where(place_row == places[q], (fb_ref[q // K] + q % K) * CB, starts)
        target = jnp.where(place_lane == places[q], owners[q] * SLOTS + slots[q], target)
    starts = jnp.where(lax.broadcasted_iota(I32, (CB, 128), 1) < 64, starts[:CB], starts[CB:])
    mine_v[...] = starts
    table_v[me_c] = starts
    stripe_of = []
    for s in range(SLOTS):
        value = jnp.int32(0)
        for q in range(K, PAIRS):
            value = value + jnp.where((owners[q] == me_g) & (slots[q] == s), 1, 0)
        stripe_of.append(value)

    raw_b[:, pl.ds(CHANNELS, 128)] = jnp.zeros((ROWS, 128), BF)
    x_v[0] = jnp.zeros((128, ROWS), BF)
    x_v[NC + 1] = jnp.zeros((128, ROWS), BF)
    lead_f[:, pl.ds(TD, 128)] = jnp.zeros((STRIPES * CB, 128), F32)

    pl.semaphore_wait(barrier, NC + NG - 2)

    def first_copy(d, peer, owner):
        return remote(mine_v, table_v.at[owner], fsend.at[d], frecv.at[d], "chan", peer)

    def send_first(d, carry):
        first_copy(d, lax.rem(me_c + d, NC), me_c).start()
        return carry

    lax.fori_loop(1, NC, send_first, 0)

    line = jnp.concatenate([taps_ref[...].reshape(1, TAPS), jnp.zeros((1, FW - TAPS), F32)], 1)
    band = pltpu.roll(jnp.broadcast_to(line, (FB, FW)), 1, 1, stride=2, stride_axis=0)
    band_hi = band.astype(BF)
    band_lo = (band - band_hi.astype(F32)).astype(BF)

    raw_in.wait()

    def round_raw(i, carry):
        at = pl.multiple_of(i * 512, 512)
        raw_b[:, pl.ds(at, 512)] = raw_v[:, pl.ds(at, 512)].astype(BF)
        return carry

    lax.fori_loop(0, CHANNELS // 512, round_raw, 0)

    ahead_by = lax.broadcasted_iota(I32, (CB, SPAN), 1) - lax.broadcasted_iota(I32, (CB, SPAN), 0)

    low = lax.broadcasted_iota(I32, (CB, 128), 1) < 64

    def packed(dst):
        base = (dst * CPD) // 128 * 128
        shift = dst * CPD - base
        both = table_v[dst]
        swapped = pltpu.roll(both, 64, 1)
        rows = [jnp.where(low, both, swapped) + shift, jnp.where(low, swapped, both) + shift]
        hot = []
        for place in range(PAIRS):
            wanted = jnp.broadcast_to(rows[place // CB][place % CB:place % CB + 1], (CB, 128))
            hot.append(jnp.where(ahead_by == jnp.concatenate([wanted] * (SPAN // 128), 1), 1.0, 0.0))
        chosen = jnp.concatenate(hot, 0).astype(BF)
        source = raw_b[:, pl.ds(pl.multiple_of(base, 128), SPAN)]
        return lax.dot_general(chosen, source, (((1,), (1,)), ((), ())), preferred_element_type=F32).astype(BF)

    def early_copy(d, dst, src):
        return remote(
            send_v.at[dst, pl.ds(0, EARLY)], x_v.at[1 + src, pl.ds(0, EARLY)], asend.at[d], arecv.at[d], "chan", dst
        )

    def late_copy(d, dst, src):
        return remote(
            send_v.at[dst, pl.ds(EARLY, 128 - EARLY)], x_v.at[1 + src, pl.ds(EARLY, 128 - EARLY)],
            bsend.at[d], brecv.at[d], "chan", dst,
        )

    def send_early(i, carry):
        dsts = [lax.rem(me_c + NC - i * PACK - j, NC) for j in range(PACK)]
        for j, dst in enumerate(dsts):

            @pl.when(i * PACK + j > 0)
            def _():
                first_copy(i * PACK + j, dst, dst).wait_recv()

        for dst, part in zip(dsts, [packed(dst) for dst in dsts]):
            send_v[dst] = part
        for j, dst in enumerate(dsts):

            @pl.when(i * PACK + j > 0)
            def _():
                early_copy(i * PACK + j, dst, me_c).start()

        return carry

    def send_late(d, carry):
        late_copy(d, lax.rem(me_c + NC - d, NC), me_c).start()
        return carry

    lax.fori_loop(0, NC // PACK, send_early, 0)
    lax.fori_loop(1, NC, send_late, 0)
    x_v[1 + me_c] = send_v[me_c]

    def wait_early(d, carry):
        peer = lax.rem(me_c + d, NC)
        early_copy(d, peer, peer).wait_recv()
        return carry

    def wait_late(d, carry):
        peer = lax.rem(me_c + d, NC)
        late_copy(d, peer, peer).wait_recv()
        return carry

    def whiten(at, count):
        window = jnp.concatenate(
            [
                jnp.concatenate([x_v[4 * block + part, pl.ds(at, count)] for part in range(FW // ROWS)], 1)
                for block in range(TD // FB)
            ],
            0,
        )
        y = sum(
            lax.dot_general(window, term, (((1,), (1,)), ((), ())), preferred_element_type=F32)
            for term in (band_hi, band_lo)
        )
        for block in range(TD // FB):
            filt[pl.ds(at, count), pl.ds(block * FB, FB)] = y[block * count:(block + 1) * count].astype(BF)

    def chosen_rows(first, count, depth):
        rows = NG * count * CB
        row_id = lax.broadcasted_iota(I32, (rows, depth), 0)
        col_id = lax.broadcasted_iota(I32, (rows, depth), 1)
        wanted = row_id // (count * CB) * SLOTS + first + row_id // CB % count
        pick = (jnp.broadcast_to(target[:, :depth], (rows, depth)) == wanted) & (row_id % CB == col_id % CB)
        rows_of = jnp.dot(
            jnp.where(pick, 1.0, 0.0).astype(BF), filt[pl.ds(0, depth)], preferred_element_type=F32
        )
        parts = [rows_of[o * count * CB:(o + 1) * count * CB] for o in range(NG)]
        return [jnp.concatenate([part[:, :HALF], part[:, HALF:]], 0).astype(BF) for part in parts]

    lax.fori_loop(1, NC, wait_early, 0)
    whiten(0, EARLY)

    right = lax.rem(me_g + 1, NG)
    left = lax.rem(me_g + NG - 1, NG)

    def lead_copy(way, hop):
        back = hop - 1 if way == 0 else NG - hop + 1
        origin = lax.rem(me_g + NG - back, NG)
        part = leads.at[origin] if hop < 4 else leads.at[origin, way]
        return remote(part, part, ls.at[way, hop - 1], lr.at[way, hop - 1], "tgroup", right if way == 0 else left)

    def lead_arrival(way, hop):
        back = hop if way == 0 else NG - hop
        origin = lax.rem(me_g + NG - back, NG)
        part = leads.at[origin] if hop < 4 else leads.at[origin, way]
        return remote(part, part, ls.at[way, hop - 1], lr.at[way, hop - 1], "tgroup", right if way == 0 else left)

    def pass_leads(hop):
        for way in range(2):
            lead_arrival(way, hop - 1).wait_recv()
            lead_copy(way, hop).start()

    for half in range(2):
        leads[me_g, half] = filt[pl.ds(0, STRIPES * CB), pl.ds(half * HALF, HALF)]
    for way in range(2):
        lead_copy(way, 1).start()

    def step_offset(i):
        return jnp.where(i % 2 == 1, (i + 1) // 2, NG - i // 2)

    def slot0_copy(i, dst, src):
        return remote(send0.at[dst], recv0.at[src], s0.at[i], r0.at[i], "tgroup", dst)

    def slot1_copy(i, dst, src):
        return remote(send1.at[dst], recv1.at[src], s1.at[i], r1.at[i], "tgroup", dst)

    def send_slot0(i, carry):
        slot0_copy(i, lax.rem(me_g + step_offset(i), NG), me_g).start()
        return carry

    def send_slot1(i, carry):
        slot1_copy(i, lax.rem(me_g + step_offset(i), NG), me_g).start()
        return carry

    for owner, part in enumerate(chosen_rows(0, 1, EARLY)):
        send0[owner] = part
    lax.fori_loop(1, NG, send_slot0, 0)
    recv0[me_g] = send0[me_g]

    def spread_leads(src):
        for half in range(2):
            lead_f[:, pl.ds(half * HALF, HALF)] = leads[src, half].astype(F32)
        for row in range(STRIPES * CB):
            line = jnp.broadcast_to(lead_f[pl.ds(row, 1)], (R, KL))
            turned = pltpu.roll(line, 0, 1, stride=1, stride_axis=0)
            shifted[src, row // CB, pl.ds(row % CB * R, R)] = turned.astype(BF)

    def correlate(src, halves, first, count, fresh=False):
        width = count * CB
        halves = halves.astype(F32)
        padded = jnp.concatenate([halves[:width], halves[width:], jnp.zeros((width, QW - TD), F32)], 1)
        turns = [pltpu.roll(padded, MAXLAG - R * step, 1) for step in range(128 // R)]
        for s in range(count):
            windows[first + s] = jnp.concatenate([turn[s * CB:(s + 1) * CB] for turn in turns], 0).astype(BF)
        for slot in range(first, first + count):
            partner = jnp.concatenate(
                [windows[slot, :, pl.ds(128 * step, KL)] for step in range(1024 // 128)], 0
            )
            product = lax.dot_general(
                partner, shifted[src, stripe_of[slot]], (((1,), (1,)), ((), ())), preferred_element_type=F32
            )
            acc[slot] = product if fresh else acc[slot] + product

    spread_leads(me_g)
    correlate(me_g, recv0[me_g], 0, 1, True)
    pass_leads(2)

    def source(i):
        return lax.rem(me_g + NG - step_offset(i), NG)

    def first_pass(i):
        src = source(i)
        spread_leads(src)
        slot0_copy(i, src, src).wait_recv()
        correlate(src, recv0[src], 0, 1)

    def ahead(i, carry):
        first_pass(i)
        return carry

    lax.fori_loop(1, 1 + AHEAD, ahead, 0)

    lax.fori_loop(1, NC, wait_late, 0)
    whiten(EARLY, 128 - EARLY)
    for owner, part in enumerate(chosen_rows(1, SLOTS - 1, 128)):
        send1[owner] = part
    lax.fori_loop(1, 3, send_slot1, 0)
    pass_leads(3)
    lax.fori_loop(3, 1 + IN_FLIGHT, send_slot1, 0)
    correlate(me_g, send1[me_g], 1, SLOTS - 1, True)

    def receive(i, carry):
        @pl.when(i + AHEAD == 5)
        def _():
            pass_leads(4)

        @pl.when(i + AHEAD == NG - 1)
        def _():
            for way in range(2):
                lead_arrival(way, 4).wait_recv()

        @pl.when(i + AHEAD < NG)
        def _():
            first_pass(i + AHEAD)

        src = source(i)
        slot1_copy(i, src, src).wait_recv()

        @pl.when(i + IN_FLIGHT < NG)
        def _():
            send_slot1(i + IN_FLIGHT, 0)

        correlate(src, recv1[src], 1, SLOTS - 1)
        return carry

    lax.fori_loop(1, NG, receive, 0)

    def wait_chan_sent(d, carry):
        dst, back = lax.rem(me_c + d, NC), lax.rem(me_c + NC - d, NC)
        first_copy(d, dst, me_c).wait_send()
        early_copy(d, back, me_c).wait_send()
        late_copy(d, back, me_c).wait_send()
        return carry

    lax.fori_loop(1, NC, wait_chan_sent, 0)

    def wait_group_sent(i, carry):
        dst = lax.rem(me_g + step_offset(i), NG)
        slot0_copy(i, dst, me_g).wait_send()
        slot1_copy(i, dst, me_g).wait_send()
        return carry

    lax.fori_loop(1, NG, wait_group_sent, 0)
    for way in range(2):
        for hop in range(1, 5):
            lead_copy(way, hop).wait_send()


def finish(acc_ref, out_ref, acc_v, out_v, in_sem, out_sem):
    scale = 1.0 / math.sqrt(TD)
    lane = lax.broadcasted_iota(I32, (CB, 128), 1)
    low, even = lane < 64, lane // R % 2 == 0

    def fetch(slot):
        return pltpu.make_async_copy(acc_ref.at[slot], acc_v.at[slot], in_sem.at[slot])

    def put(slot):
        return pltpu.make_async_copy(out_v.at[slot], out_ref.at[slot], out_sem.at[slot])

    for slot in range(SLOTS):
        fetch(slot).start()

    def one_slot(slot, carry):
        fetch(slot).wait()
        for step in range(1024 // 128):
            for half in range(2):
                p = [
                    acc_v[slot, pl.ds(step * 4 * CB + s * CB, CB), pl.ds(half * 128, 128)] * scale for s in range(4)
                ]
                far = [None] * 4
                for s in range(2):
                    far[s] = jnp.where(low, p[s], pltpu.roll(p[s + 2], 64, 1))
                    far[s + 2] = jnp.where(low, pltpu.roll(p[s], 64, 1), p[s + 2])
                width = min(128, LAGS - step * 128)
                for s in (0, 2):
                    first = jnp.where(even, far[s], pltpu.roll(far[s + 1], R, 1))
                    second = jnp.where(even, pltpu.roll(far[s], 128 - R, 1), far[s + 1])
                    out_v[slot, half * 4 + s, :, pl.ds(step * 128, width)] = first[:, :width]
                    out_v[slot, half * 4 + s + 1, :, pl.ds(step * 128, width)] = second[:, :width]
        put(slot).start()
        return carry

    lax.fori_loop(0, SLOTS, one_slot, 0)
    for slot in range(SLOTS):
        put(slot).wait()


def local(raw_strain, whitening_taps, first_block, pair_owner):
    vmem = pl.BlockSpec(memory_space=pltpu.VMEM)
    smem = pl.BlockSpec(memory_space=pltpu.SMEM)
    dma = pltpu.SemaphoreType.DMA
    acc = pl.pallas_call(
        kernel,
        out_shape=jax.ShapeDtypeStruct((SLOTS, 256, 256), F32),
        in_specs=[pl.BlockSpec(memory_space=pl.ANY), vmem, smem, smem],
        out_specs=vmem,
        scratch_shapes=[
            pltpu.VMEM((ROWS, CHANNELS), F32),
            pltpu.VMEM((ROWS, WIDE), BF),
            pltpu.VMEM((NC, CB, 128), I32),
            pltpu.VMEM((CB, 128), I32),
            pltpu.VMEM((NC, 128, ROWS), BF),
            pltpu.VMEM((NC + 2, 128, ROWS), BF),
            pltpu.VMEM((128, TD), BF),
            pltpu.VMEM((NG, 2 * CB, HALF), BF),
            pltpu.VMEM((NG, 2 * CB, HALF), BF),
            pltpu.VMEM((NG, 2 * CB * (SLOTS - 1), HALF), BF),
            pltpu.VMEM((NG, 2 * CB * (SLOTS - 1), HALF), BF),
            pltpu.VMEM((NG, 2, STRIPES * CB, HALF), BF),
            pltpu.VMEM((STRIPES * CB, KL), F32),
            pltpu.VMEM((NG, STRIPES, CB * R, KL), BF),
            pltpu.VMEM((SLOTS, 4 * CB, QW), BF),
            dma, dma((NC,)), dma((NC,)), dma((NC,)), dma((NC,)), dma((NC,)), dma((NC,)),
            dma((NG,)), dma((NG,)), dma((NG,)), dma((NG,)), dma((2, 4)), dma((2, 4)),
        ],
        compiler_params=pltpu.CompilerParams(
            collective_id=0, has_side_effects=True, vmem_limit_bytes=56 << 20
        ),
        cost_estimate=pl.CostEstimate(flops=12 << 30, bytes_accessed=8 << 20, transcendentals=0),
    )(raw_strain, whitening_taps, first_block, pair_owner.reshape(PAIRS))
    return pl.pallas_call(
        finish,
        out_shape=jax.ShapeDtypeStruct((SLOTS, CB, CB, LAGS), F32),
        in_specs=[pl.BlockSpec(memory_space=pltpu.HBM)],
        out_specs=pl.BlockSpec(memory_space=pltpu.HBM),
        scratch_shapes=[
            pltpu.VMEM((SLOTS, 256, 256), F32), pltpu.VMEM((SLOTS, CB, CB, LAGS), F32), dma((SLOTS,)), dma((SLOTS,)),
        ],
    )(acc)


def solution(mesh):
    in_specs = (P(("tgroup", "chan"), None), P(), P("chan"), P("chan", None))
    out_specs = P(("tgroup", "chan"), None, None, None)
    return jax.shard_map(local, mesh=mesh, in_specs=in_specs, out_specs=out_specs, check_vma=False)
```

```python
import math

import jax
import jax.numpy as jnp
from jax import lax
from jax.experimental import pallas as pl
from jax.experimental.pallas import tpu as pltpu
from jax.sharding import PartitionSpec as P

MESH = pl.DeviceIdType.MESH
MAXLAG = 500
LAGS = 1001
CB = 8
K = 8
STRIPES = 2
SLOTS = 5
TAPS = 255
NG = 8
NC = 32
CPD = 320
CHANNELS = 10240
ROWS = 128
TS = 4096
TD = 2048
HALF = TD // 2
PAIRS = STRIPES * K
WIDE = CHANNELS + 128
SPAN = 512
EARLY = 80
PACK = 4
AHEAD = 2
IN_FLIGHT = 4
FB = 256
FW = 768
R = 32
KL = TD + 128
QW = TD + 1024
F32 = jnp.float32
BF = jnp.bfloat16
I32 = jnp.int32


def remote(src, dst, send_sem, recv_sem, axis, target):
    return pltpu.make_async_remote_copy(
        src_ref=src, dst_ref=dst, send_sem=send_sem, recv_sem=recv_sem,
        device_id={axis: target}, device_id_type=MESH,
    )


def kernel(
    raw_ref, taps_ref, fb_ref, owner_ref, acc,
    raw_v, raw_b, table_v, mine_v, send_v, x_v, filt, send0, recv0, send1, recv1, leads, lead_f, shifted, windows,
    raw_sem, fsend, frecv, asend, arecv, bsend, brecv, s0, r0, s1, r1, ls, lr,
):
    me_c = lax.axis_index("chan")
    me_g = lax.axis_index("tgroup")

    barrier = pltpu.get_barrier_semaphore()

    def greet_chan(d, carry):
        pl.semaphore_signal(barrier, inc=1, device_id={"chan": lax.rem(me_c + d, NC)}, device_id_type=MESH)
        return carry

    def greet_group(d, carry):
        pl.semaphore_signal(barrier, inc=1, device_id={"tgroup": lax.rem(me_g + d, NG)}, device_id_type=MESH)
        return carry

    lax.fori_loop(1, NC, greet_chan, 0)
    lax.fori_loop(1, NG, greet_group, 0)
    raw_in = pltpu.make_async_copy(raw_ref, raw_v, raw_sem)
    raw_in.start()

    owners = [owner_ref[q] for q in range(PAIRS)]
    slots = []
    for q in range(PAIRS):
        count = jnp.int32(0)
        for earlier in range(q):
            count = count + jnp.where(owners[earlier] == owners[q], 1, 0)
        slots.append(count)
    keys = [jnp.int32(q // K - 2) if q % K == 0 else slots[q] * PAIRS + q for q in range(PAIRS)]
    places = [jnp.int32(0)] * PAIRS
    for q in range(PAIRS):
        for other in range(q):
            ahead = jnp.where(keys[other] < keys[q], 1, 0)
            places[q] = places[q] + ahead
            places[other] = places[other] + 1 - ahead
    place_row = lax.broadcasted_iota(I32, (PAIRS, 128), 0)
    place_lane = lax.broadcasted_iota(I32, (1, 128), 1) // CB
    starts = jnp.zeros((PAIRS, 128), I32)
    target = jnp.zeros((1, 128), I32)
    for q in range(PAIRS):
        starts = jnp.where(place_row == places[q], (fb_ref[q // K] + q % K) * CB, starts)
        target = jnp.where(place_lane == places[q], owners[q] * SLOTS + slots[q], target)
    starts = jnp.where(lax.broadcasted_iota(I32, (CB, 128), 1) < 64, starts[:CB], starts[CB:])
    mine_v[...] = starts
    table_v[me_c] = starts
    stripe_of = []
    for s in range(SLOTS):
        value = jnp.int32(0)
        for q in range(K, PAIRS):
            value = value + jnp.where((owners[q] == me_g) & (slots[q] == s), 1, 0)
        stripe_of.append(value)

    raw_b[:, pl.ds(CHANNELS, 128)] = jnp.zeros((ROWS, 128), BF)
    x_v[0] = jnp.zeros((128, ROWS), BF)
    x_v[NC + 1] = jnp.zeros((128, ROWS), BF)
    lead_f[:, pl.ds(TD, 128)] = jnp.zeros((STRIPES * CB, 128), F32)

    pl.semaphore_wait(barrier, NC + NG - 2)

    def first_copy(d, peer, owner):
        return remote(mine_v, table_v.at[owner], fsend.at[d], frecv.at[d], "chan", peer)

    def send_first(d, carry):
        first_copy(d, lax.rem(me_c + d, NC), me_c).start()
        return carry

    lax.fori_loop(1, NC, send_first, 0)

    line = jnp.concatenate([taps_ref[...].reshape(1, TAPS), jnp.zeros((1, FW - TAPS), F32)], 1)
    band = pltpu.roll(jnp.broadcast_to(line, (FB, FW)), 1, 1, stride=2, stride_axis=0)
    band_hi = band.astype(BF)
    band_lo = (band - band_hi.astype(F32)).astype(BF)

    raw_in.wait()

    def round_raw(i, carry):
        at = pl.multiple_of(i * 512, 512)
        raw_b[:, pl.ds(at, 512)] = raw_v[:, pl.ds(at, 512)].astype(BF)
        return carry

    lax.fori_loop(0, CHANNELS // 512, round_raw, 0)

    ahead_by = lax.broadcasted_iota(I32, (CB, SPAN), 1) - lax.broadcasted_iota(I32, (CB, SPAN), 0)

    low = lax.broadcasted_iota(I32, (CB, 128), 1) < 64

    def packed(dst):
        base = (dst * CPD) // 128 * 128
        shift = dst * CPD - base
        both = table_v[dst]
        swapped = pltpu.roll(both, 64, 1)
        rows = [jnp.where(low, both, swapped) + shift, jnp.where(low, swapped, both) + shift]
        hot = []
        for place in range(PAIRS):
            wanted = jnp.broadcast_to(rows[place // CB][place % CB:place % CB + 1], (CB, 128))
            hot.append(jnp.where(ahead_by == jnp.concatenate([wanted] * (SPAN // 128), 1), 1.0, 0.0))
        chosen = jnp.concatenate(hot, 0).astype(BF)
        source = raw_b[:, pl.ds(pl.multiple_of(base, 128), SPAN)]
        return lax.dot_general(chosen, source, (((1,), (1,)), ((), ())), preferred_element_type=F32).astype(BF)

    def early_copy(d, dst, src):
        return remote(
            send_v.at[dst, pl.ds(0, EARLY)], x_v.at[1 + src, pl.ds(0, EARLY)], asend.at[d], arecv.at[d], "chan", dst
        )

    def late_copy(d, dst, src):
        return remote(
            send_v.at[dst, pl.ds(EARLY, 128 - EARLY)], x_v.at[1 + src, pl.ds(EARLY, 128 - EARLY)],
            bsend.at[d], brecv.at[d], "chan", dst,
        )

    def send_early(i, carry):
        dsts = [lax.rem(me_c + NC - i * PACK - j, NC) for j in range(PACK)]
        for j, dst in enumerate(dsts):

            @pl.when(i * PACK + j > 0)
            def _():
                first_copy(i * PACK + j, dst, dst).wait_recv()

        for dst, part in zip(dsts, [packed(dst) for dst in dsts]):
            send_v[dst] = part
        for j, dst in enumerate(dsts):

            @pl.when(i * PACK + j > 0)
            def _():
                early_copy(i * PACK + j, dst, me_c).start()

        return carry

    def send_late(d, carry):
        late_copy(d, lax.rem(me_c + NC - d, NC), me_c).start()
        return carry

    lax.fori_loop(0, NC // PACK, send_early, 0)
    lax.fori_loop(1, NC, send_late, 0)
    x_v[1 + me_c] = send_v[me_c]

    def wait_early(d, carry):
        peer = lax.rem(me_c + d, NC)
        early_copy(d, peer, peer).wait_recv()
        return carry

    def wait_late(d, carry):
        peer = lax.rem(me_c + d, NC)
        late_copy(d, peer, peer).wait_recv()
        return carry

    def whiten(at, count):
        window = jnp.concatenate(
            [
                jnp.concatenate([x_v[4 * block + part, pl.ds(at, count)] for part in range(FW // ROWS)], 1)
                for block in range(TD // FB)
            ],
            0,
        )
        y = sum(
            lax.dot_general(window, term, (((1,), (1,)), ((), ())), preferred_element_type=F32)
            for term in (band_hi, band_lo)
        )
        for block in range(TD // FB):
            filt[pl.ds(at, count), pl.ds(block * FB, FB)] = y[block * count:(block + 1) * count].astype(BF)

    def chosen_rows(first, count, depth):
        rows = NG * count * CB
        row_id = lax.broadcasted_iota(I32, (rows, depth), 0)
        col_id = lax.broadcasted_iota(I32, (rows, depth), 1)
        wanted = row_id // (count * CB) * SLOTS + first + row_id // CB % count
        pick = (jnp.broadcast_to(target[:, :depth], (rows, depth)) == wanted) & (row_id % CB == col_id % CB)
        rows_of = jnp.dot(
            jnp.where(pick, 1.0, 0.0).astype(BF), filt[pl.ds(0, depth)], preferred_element_type=F32
        )
        parts = [rows_of[o * count * CB:(o + 1) * count * CB] for o in range(NG)]
        return [jnp.concatenate([part[:, :HALF], part[:, HALF:]], 0).astype(BF) for part in parts]

    lax.fori_loop(1, NC, wait_early, 0)
    whiten(0, EARLY)

    right = lax.rem(me_g + 1, NG)
    left = lax.rem(me_g + NG - 1, NG)

    def lead_copy(way, hop):
        back = hop - 1 if way == 0 else NG - hop + 1
        origin = lax.rem(me_g + NG - back, NG)
        part = leads.at[origin] if hop < 4 else leads.at[origin, way]
        return remote(part, part, ls.at[way, hop - 1], lr.at[way, hop - 1], "tgroup", right if way == 0 else left)

    def lead_arrival(way, hop):
        back = hop if way == 0 else NG - hop
        origin = lax.rem(me_g + NG - back, NG)
        part = leads.at[origin] if hop < 4 else leads.at[origin, way]
        return remote(part, part, ls.at[way, hop - 1], lr.at[way, hop - 1], "tgroup", right if way == 0 else left)

    def pass_leads(hop):
        for way in range(2):
            lead_arrival(way, hop - 1).wait_recv()
            lead_copy(way, hop).start()

    for half in range(2):
        leads[me_g, half] = filt[pl.ds(0, STRIPES * CB), pl.ds(half * HALF, HALF)]
    for way in range(2):
        lead_copy(way, 1).start()

    def step_offset(i):
        return jnp.where(i % 2 == 1, (i + 1) // 2, NG - i // 2)

    def slot0_copy(i, dst, src):
        return remote(send0.at[dst], recv0.at[src], s0.at[i], r0.at[i], "tgroup", dst)

    def slot1_copy(i, dst, src):
        return remote(send1.at[dst], recv1.at[src], s1.at[i], r1.at[i], "tgroup", dst)

    def send_slot0(i, carry):
        slot0_copy(i, lax.rem(me_g + step_offset(i), NG), me_g).start()
        return carry

    def send_slot1(i, carry):
        slot1_copy(i, lax.rem(me_g + step_offset(i), NG), me_g).start()
        return carry

    for owner, part in enumerate(chosen_rows(0, 1, EARLY)):
        send0[owner] = part
    lax.fori_loop(1, NG, send_slot0, 0)
    recv0[me_g] = send0[me_g]

    def spread_leads(src):
        for half in range(2):
            lead_f[:, pl.ds(half * HALF, HALF)] = leads[src, half].astype(F32)
        for row in range(STRIPES * CB):
            line = jnp.broadcast_to(lead_f[pl.ds(row, 1)], (R, KL))
            turned = pltpu.roll(line, 0, 1, stride=1, stride_axis=0)
            shifted[src, row // CB, pl.ds(row % CB * R, R)] = turned.astype(BF)

    def correlate(src, halves, first, count, fresh=False):
        width = count * CB
        halves = halves.astype(F32)
        padded = jnp.concatenate([halves[:width], halves[width:], jnp.zeros((width, QW - TD), F32)], 1)
        turns = [pltpu.roll(padded, MAXLAG - R * step, 1) for step in range(128 // R)]
        for s in range(count):
            windows[first + s] = jnp.concatenate([turn[s * CB:(s + 1) * CB] for turn in turns], 0).astype(BF)
        for slot in range(first, first + count):
            partner = jnp.concatenate(
                [windows[slot, :, pl.ds(128 * step, KL)] for step in range(1024 // 128)], 0
            )
            product = lax.dot_general(
                partner, shifted[src, stripe_of[slot]], (((1,), (1,)), ((), ())), preferred_element_type=F32
            )
            acc[slot] = product if fresh else acc[slot] + product

    spread_leads(me_g)
    correlate(me_g, recv0[me_g], 0, 1, True)
    pass_leads(2)

    def source(i):
        return lax.rem(me_g + NG - step_offset(i), NG)

    def first_pass(i):
        src = source(i)
        spread_leads(src)
        slot0_copy(i, src, src).wait_recv()
        correlate(src, recv0[src], 0, 1)

    def ahead(i, carry):
        first_pass(i)
        return carry

    lax.fori_loop(1, 1 + AHEAD, ahead, 0)

    lax.fori_loop(1, NC, wait_late, 0)
    whiten(EARLY, 128 - EARLY)
    for owner, part in enumerate(chosen_rows(1, SLOTS - 1, 128)):
        send1[owner] = part
    lax.fori_loop(1, 3, send_slot1, 0)
    pass_leads(3)
    lax.fori_loop(3, 1 + IN_FLIGHT, send_slot1, 0)
    correlate(me_g, send1[me_g], 1, SLOTS - 1, True)

    def receive(i, carry):
        @pl.when(i + AHEAD == 5)
        def _():
            pass_leads(4)

        @pl.when(i + AHEAD == NG - 1)
        def _():
            for way in range(2):
                lead_arrival(way, 4).wait_recv()

        @pl.when(i + AHEAD < NG)
        def _():
            first_pass(i + AHEAD)

        src = source(i)
        slot1_copy(i, src, src).wait_recv()

        @pl.when(i + IN_FLIGHT < NG)
        def _():
            send_slot1(i + IN_FLIGHT, 0)

        correlate(src, recv1[src], 1, SLOTS - 1)
        return carry

    lax.fori_loop(1, NG, receive, 0)

    def wait_chan_sent(d, carry):
        dst, back = lax.rem(me_c + d, NC), lax.rem(me_c + NC - d, NC)
        first_copy(d, dst, me_c).wait_send()
        early_copy(d, back, me_c).wait_send()
        late_copy(d, back, me_c).wait_send()
        return carry

    lax.fori_loop(1, NC, wait_chan_sent, 0)

    def wait_group_sent(i, carry):
        dst = lax.rem(me_g + step_offset(i), NG)
        slot0_copy(i, dst, me_g).wait_send()
        slot1_copy(i, dst, me_g).wait_send()
        return carry

    lax.fori_loop(1, NG, wait_group_sent, 0)
    for way in range(2):
        for hop in range(1, 5):
            lead_copy(way, hop).wait_send()


def finish(acc_ref, out_ref, acc_v, out_v, in_sem, out_sem):
    scale = 1.0 / math.sqrt(TD)
    lane = lax.broadcasted_iota(I32, (CB, 128), 1)
    low, even = lane < 64, lane // R % 2 == 0

    def fetch(slot):
        return pltpu.make_async_copy(acc_ref.at[slot], acc_v.at[slot], in_sem.at[slot])

    def put(slot):
        return pltpu.make_async_copy(out_v.at[slot], out_ref.at[slot], out_sem.at[slot])

    for slot in range(SLOTS):
        fetch(slot).start()

    def one_slot(slot, carry):
        fetch(slot).wait()
        for step in range(1024 // 128):
            for half in range(2):
                p = [
                    acc_v[slot, pl.ds(step * 4 * CB + s * CB, CB), pl.ds(half * 128, 128)] * scale for s in range(4)
                ]
                far = [None] * 4
                for s in range(2):
                    far[s] = jnp.where(low, p[s], pltpu.roll(p[s + 2], 64, 1))
                    far[s + 2] = jnp.where(low, pltpu.roll(p[s], 64, 1), p[s + 2])
                width = min(128, LAGS - step * 128)
                for s in (0, 2):
                    first = jnp.where(even, far[s], pltpu.roll(far[s + 1], R, 1))
                    second = jnp.where(even, pltpu.roll(far[s], 128 - R, 1), far[s + 1])
                    out_v[slot, half * 4 + s, :, pl.ds(step * 128, width)] = first[:, :width]
                    out_v[slot, half * 4 + s + 1, :, pl.ds(step * 128, width)] = second[:, :width]
        put(slot).start()
        return carry

    lax.fori_loop(0, SLOTS, one_slot, 0)
    for slot in range(SLOTS):
        put(slot).wait()


def local(raw_strain, whitening_taps, first_block, pair_owner):
    vmem = pl.BlockSpec(memory_space=pltpu.VMEM)
    smem = pl.BlockSpec(memory_space=pltpu.SMEM)
    dma = pltpu.SemaphoreType.DMA
    acc = pl.pallas_call(
        kernel,
        out_shape=jax.ShapeDtypeStruct((SLOTS, 256, 256), F32),
        in_specs=[pl.BlockSpec(memory_space=pl.ANY), vmem, smem, smem],
        out_specs=vmem,
        scratch_shapes=[
            pltpu.VMEM((ROWS, CHANNELS), F32),
            pltpu.VMEM((ROWS, WIDE), BF),
            pltpu.VMEM((NC, CB, 128), I32),
            pltpu.VMEM((CB, 128), I32),
            pltpu.VMEM((NC, 128, ROWS), BF),
            pltpu.VMEM((NC + 2, 128, ROWS), BF),
            pltpu.VMEM((128, TD), BF),
            pltpu.VMEM((NG, 2 * CB, HALF), BF),
            pltpu.VMEM((NG, 2 * CB, HALF), BF),
            pltpu.VMEM((NG, 2 * CB * (SLOTS - 1), HALF), BF),
            pltpu.VMEM((NG, 2 * CB * (SLOTS - 1), HALF), BF),
            pltpu.VMEM((NG, 2, STRIPES * CB, HALF), BF),
            pltpu.VMEM((STRIPES * CB, KL), F32),
            pltpu.VMEM((NG, STRIPES, CB * R, KL), BF),
            pltpu.VMEM((SLOTS, 4 * CB, QW), BF),
            dma, dma((NC,)), dma((NC,)), dma((NC,)), dma((NC,)), dma((NC,)), dma((NC,)),
            dma((NG,)), dma((NG,)), dma((NG,)), dma((NG,)), dma((2, 4)), dma((2, 4)),
        ],
        compiler_params=pltpu.CompilerParams(
            collective_id=0, has_side_effects=True, vmem_limit_bytes=56 << 20
        ),
        cost_estimate=pl.CostEstimate(flops=12 << 30, bytes_accessed=8 << 20, transcendentals=0),
    )(raw_strain, whitening_taps, first_block, pair_owner.reshape(PAIRS))
    return pl.pallas_call(
        finish,
        out_shape=jax.ShapeDtypeStruct((SLOTS, CB, CB, LAGS), F32),
        in_specs=[pl.BlockSpec(memory_space=pltpu.HBM)],
        out_specs=pl.BlockSpec(memory_space=pltpu.HBM),
        scratch_shapes=[
            pltpu.VMEM((SLOTS, 256, 256), F32), pltpu.VMEM((SLOTS, CB, CB, LAGS), F32), dma((SLOTS,)), dma((SLOTS,)),
        ],
    )(acc)


def solution(mesh):
    in_specs = (P(("tgroup", "chan"), None), P(), P("chan"), P("chan", None))
    out_specs = P(("tgroup", "chan"), None, None, None)
    return jax.shard_map(local, mesh=mesh, in_specs=in_specs, out_specs=out_specs, check_vma=False)
```
